128 devices in a mesh: ctx: 16 (over y, z_hi, core), head: 8 (over z_lo, x).
Axes of the slice: x: 4, y: 4, z: 4 (z_hi: 2, z_lo: 2; z = z_hi * 2 + z_lo), core: 2. Of those that a mesh axis runs over, the one named last changes fastest.
Arguments:
- queries: bfloat16 [8192, 4096], P('ctx', 'head'), may hold values from -160 to 160
- key_input: bfloat16 [8192, 1024], P('ctx', 'head'), may hold values from -24 to 24
- value_input: bfloat16 [8192, 1024], P('ctx', 'head'), may hold values from -6 to 6
- out_weight: bfloat16 [4096, 4096], P(None, 'head'), may hold values from -0.09375 to 0.09375
- lengths: int32 [6], replicated, may hold values from 1 to 6144, 8192 in all
- grad_projected: bfloat16 [8192, 4096], P('ctx', 'head'), may hold values from -6 to 6
Outputs:
- projected: bfloat16 [8192, 4096], P('ctx', 'head')
- query_grads: bfloat16 [8192, 4096], P('ctx', 'head')
- key_grads: bfloat16 [8192, 1024], P('ctx', 'head')
- value_grads: bfloat16 [8192, 1024], P('ctx', 'head')
The draws below stay inside these ranges and needn't reach their ends.
Inputs may be any that keep to these rules, and one draw needn't show every extreme that they name: `lengths`: they sum to 8192.
All inputs are finite; a program needn't handle non-finite values.
Results may differ from the reference program's by a relative error of at most 0.035.
Values may be sent and summed in bfloat16 or wider, within the bound.
A program may use at most 128 MiB of HBM per device.

```python
import math
import jax
import jax.numpy as jnp
import numpy as np
from jax import lax

D = 4096
QH = 32
KVH = 8
HD = 128
DOCS = 6
TOKENS = 8192
LONGEST = 6144
N_HEAD = 8


def shared_rows(key):
    base = jnp.clip(jax.random.normal(key, (TOKENS, KVH, HD), jnp.float32), -6.0, 6.0)
    return base


def draw_key_input(key, part):
    base = shared_rows(key)
    rows = base
    return rows.reshape(TOKENS, KVH * HD).astype(jnp.bfloat16)


def draw_queries(key, part):
    key = jax.random.fold_in(key, 5)
    rows = jnp.clip(jax.random.normal(key, (TOKENS, QH, HD), jnp.float32), -6.0, 6.0)
    return rows.reshape(TOKENS, QH * HD).astype(jnp.bfloat16)


def block_levels(rng, extent, split, least, largest):
    loudness, own = 1.0, jax.random.fold_in(rng, 6)
    for dim, shards_of in split:
        steps = jnp.exp(jax.random.uniform(jax.random.fold_in(own, dim), (shards_of,), jnp.float32, least / len(split), largest / len(split)))
        loudness = loudness * jnp.repeat(steps, extent[dim] // shards_of).reshape([-1 if axis == dim else 1 for axis in range(len(extent))])
    return loudness


def length_profile(number_of, total, most, lean):
    weights = [(1 << 20) // math.isqrt(grade ** lean) + 1 for grade in range(2, number_of + 1)]
    rest, given = total - most - (number_of - 1), [1] * (number_of - 1)
    while rest > 0:
        free = [i for i in range(number_of - 1) if given[i] < most]
        mass, left = sum([weights[i] for i in free]), rest
        for i in free:
            more = min(most - given[i], max(1, left * weights[i] // mass), rest)
            given[i] = given[i] + more
            rest = rest - more
    return np.array([most] + given)


def ragged(rng, amount, total, bound, slope):
    if amount == 2:
        one = jax.random.randint(rng, (), max(1, total - bound), min(bound, total - 1) + 1)
        return jnp.stack([one, total - one])
    tallies = jnp.asarray(length_profile(amount, total, bound, slope), jnp.int32)
    twos = (amount - 1) // 2
    donor, taker = tallies[1:1 + 2 * twos:2], tallies[2:2 + 2 * twos:2]
    room = jnp.minimum(donor - 1, bound - taker)
    shifted = jax.random.randint(jax.random.fold_in(rng, 1), (twos,), 0, 1 << 20) % (room + 1)
    tallies = tallies.at[1:1 + 2 * twos:2].set(donor - shifted).at[2:2 + 2 * twos:2].set(taker + shifted)
    return tallies[jax.random.permutation(jax.random.fold_in(rng, 2), amount)]


def noise(rng, extent, scale, bound, pieces=(), kind=jnp.bfloat16):
    factor_of = block_levels(rng, extent, pieces, -0.22, 0.18) if pieces else 1.0
    result = jax.random.normal(rng, extent, jnp.float32) * scale * factor_of
    return jnp.minimum(jnp.maximum(result, -bound), bound).astype(kind)


def setup_inputs(seed: int = 0) -> dict:
    seeds = jax.random.split(jax.random.key(seed), 7)
    queries = draw_queries(jax.random.fold_in(seeds[6], 71), 0)
    key_input = draw_key_input(jax.random.fold_in(seeds[6], 71), 0)
    value_input = noise(seeds[2], (TOKENS, KVH * HD), 1.0, 6.0, ((0, 16), (1, 8)))
    out_weight = noise(seeds[3], (QH * HD, D), (QH * HD) ** -0.5, 0.09375, ((1, 8),))
    lengths = ragged(seeds[4], DOCS, TOKENS, LONGEST, 1).astype(jnp.int32)
    grad_projected = noise(seeds[5], (TOKENS, D), 1.0, 6.0, ((0, 16), (1, 8)))
    return {"queries": queries, "key_input": key_input, "value_input": value_input, "out_weight": out_weight, "lengths": lengths, "grad_projected": grad_projected}


neg_big = -1e+30

def doc_starts(lengths, positions):
    ends = jnp.cumsum(lengths).astype(jnp.int32)
    starts = (ends - lengths).astype(jnp.int32)
    inside = starts[None, :] <= positions[:, None]
    return lax.optimization_barrier(jnp.max(jnp.where(inside, starts[None, :], 0), axis=1)).astype(jnp.int32)

def reference(queries, key_input, value_input, out_weight, lengths, grad_projected):
    tokens_all = queries.shape[0]
    per_group = QH // KVH
    inv_root = 1.0 / math.sqrt(HD)
    positions = jnp.arange(tokens_all, dtype=jnp.int32)
    starts_of = doc_starts(lengths, positions)
    visible = (positions[None, :] <= positions[:, None]) & (positions[None, :] >= starts_of[:, None])
    group_cols = D // N_HEAD
    grad_sum = jnp.zeros((tokens_all, QH * HD), jnp.float32)
    for group_index in range(N_HEAD):
        grad_cols = grad_projected[:, group_index * group_cols:(group_index + 1) * group_cols]
        weight_cols = out_weight[:, group_index * group_cols:(group_index + 1) * group_cols]
        grad_part = jnp.dot(grad_cols, weight_cols.T, preferred_element_type=jnp.float32)
        rounded = lax.optimization_barrier(grad_part.astype(jnp.bfloat16))
        grad_sum = grad_sum + rounded.astype(jnp.float32)
    attention_grads = grad_sum.astype(jnp.bfloat16)
    query_heads = queries.reshape(tokens_all, QH, HD).transpose(1, 0, 2)
    key_heads = jnp.repeat(key_input.reshape(tokens_all, KVH, HD).transpose(1, 0, 2), per_group, axis=0)
    value_heads = jnp.repeat(value_input.reshape(tokens_all, KVH, HD).transpose(1, 0, 2), per_group, axis=0)
    grad_heads = attention_grads.reshape(tokens_all, QH, HD).transpose(1, 0, 2)

    def one_head(operands):
        query_rows, key_rows, value_rows, grad_rows = operands
        scores = jnp.dot(query_rows, key_rows.T, preferred_element_type=jnp.float32) * inv_root
        masked = jnp.where(visible, scores, neg_big)
        row_max = lax.optimization_barrier(jnp.max(masked, axis=1))
        weights = jnp.where(visible, jnp.exp(masked - row_max[:, None]), 0.0)
        row_total = lax.optimization_barrier(jnp.sum(weights, axis=1))
        log_total = row_max + jnp.log(row_total)
        attended = (jnp.dot(weights.astype(jnp.bfloat16), value_rows, preferred_element_type=jnp.float32) / row_total[:, None]).astype(jnp.bfloat16)
        attended = lax.optimization_barrier(attended)
        row_delta = lax.optimization_barrier(jnp.sum(grad_rows.astype(jnp.float32) * attended.astype(jnp.float32), axis=1))
        probs = jnp.where(visible, jnp.exp(masked - log_total[:, None]), 0.0)
        dprobs = jnp.dot(grad_rows, value_rows.T, preferred_element_type=jnp.float32)
        dscores = (probs * (dprobs - row_delta[:, None])).astype(jnp.bfloat16)
        query_grad = jnp.dot(dscores, key_rows, preferred_element_type=jnp.float32) * inv_root
        key_grad = jnp.dot(dscores.T, query_rows, preferred_element_type=jnp.float32) * inv_root
        value_grad = jnp.dot(probs.astype(jnp.bfloat16).T, grad_rows, preferred_element_type=jnp.float32)
        return (attended, query_grad, key_grad, value_grad)
    attended, query_grad, key_grad, value_grad = lax.map(one_head, (query_heads, key_heads, value_heads, grad_heads))
    attention = attended.transpose(1, 0, 2).reshape(tokens_all, QH * HD)
    projected = jnp.dot(attention, out_weight, preferred_element_type=jnp.float32).astype(jnp.bfloat16)
    query_grads = query_grad.transpose(1, 0, 2).reshape(tokens_all, QH * HD).astype(jnp.bfloat16)
    key_grads = key_grad.reshape(KVH, per_group, tokens_all, HD).sum(axis=1).transpose(1, 0, 2).reshape(tokens_all, KVH * HD).astype(jnp.bfloat16)
    value_grads = value_grad.reshape(KVH, per_group, tokens_all, HD).sum(axis=1).transpose(1, 0, 2).reshape(tokens_all, KVH * HD).astype(jnp.bfloat16)
    return (projected, query_grads, key_grads, value_grads)
```

```python
import math

import jax
import jax.numpy as jnp
from jax import lax
from jax.experimental import pallas as pl
from jax.experimental.pallas import tpu as pltpu
from jax.sharding import PartitionSpec as P

HD = 128
GROUP = 4
ROWS = 512
CHUNK = 128
CTX = 16
TOKENS = 8192
INV_ROOT = 1.0 / math.sqrt(HD)
TO_LOG2 = INV_ROOT * math.log2(math.e)
LOWEST = -1e30
FIRST = 384
MESH = pl.DeviceIdType.MESH
BF = jnp.bfloat16
F32 = jnp.float32


def coords():
    c = lax.axis_index("ctx")
    h = lax.axis_index("head")
    y = lax.div(c, 4)
    zh = lax.rem(lax.div(c, 2), 2)
    core = lax.rem(c, 2)
    zl = lax.div(h, 4)
    x = lax.rem(h, 4)
    return y, zh, core, zl, x


def device(y, zh, core, zl, x):
    return {"ctx": y * 4 + zh * 2 + core, "head": zl * 4 + x}


def around(i):
    return lax.rem(i + 4, 4)


def source_of(slot, y, zh, core):
    if slot % 2 == 0:
        return slot, zh, core, y
    return slot, zh, 1 - core, 3 - y


class Copies:
    def __init__(self, send, recv):
        self.send, self.recv = send, recv
        self.made = []
        self.next = 0

    def new(self, src, dst, dev):
        i = self.next
        self.next += 1
        copy = pltpu.make_async_remote_copy(
            src_ref=src,
            dst_ref=dst,
            send_sem=self.send.at[i],
            recv_sem=self.recv.at[i],
            device_id=dev,
            device_id_type=MESH,
        )
        self.made.append(copy)
        return copy

    def go(self, src, dst, dev):
        copy = self.new(src, dst, dev)
        copy.start()
        return copy

    def finish_sends(self):
        for copy in self.made:
            copy.wait_send()


def greet(y, zh, core, zl, x):
    barrier = pltpu.get_barrier_semaphore()
    c = y * 4 + zh * 2 + core
    peers = [device(y, zh, core, zl, around(x + 1)), device(y, zh, core, zl, around(x - 1)), device(y, zh, core, 1 - zl, x)]
    for step in range(1, CTX):
        peers.append({"ctx": lax.rem(c + step, CTX), "head": zl * 4 + x})
    for peer in peers:
        pl.semaphore_signal(barrier, inc=1, device_id=peer, device_id_type=MESH)
    pl.semaphore_wait(barrier, len(peers))


def deal_out(src, dst, sems, where):
    y, zh, core, zl, x = where
    send, recv = sems
    odd = lax.rem(y, 2)
    copies = []
    for r in range(4):
        copy = pltpu.make_async_remote_copy(
            src_ref=src.at[pl.ds(r * CHUNK, CHUNK), :],
            dst_ref=dst.at[pl.ds(y * CHUNK, CHUNK), :],
            send_sem=send.at[r],
            recv_sem=recv.at[y],
            device_id=device(r + odd * (3 - 2 * r), zh, core + odd * (1 - 2 * core), zl, x),
            device_id_type=MESH,
        )
        copies.append(copy)
    return copies


def deal_start(copies, r, where):
    y = where[0]
    mine = jnp.logical_and(lax.rem(y, 2) == 0, y == r)

    @pl.when(jnp.logical_not(mine))
    def _():
        copies[r].start()


def deal_keep(src, dst, where):
    y = where[0]

    @pl.when(lax.rem(y, 2) == 0)
    def _():
        rows = pl.ds(y * CHUNK, CHUNK)
        dst[rows, :] = src[rows, :]


def deal_wait(src, dst, sems, where):
    y, zh, core, zl, x = where
    send, recv = sems
    for r in range(4):
        for kind in (0, 1):
            mine = jnp.logical_and(lax.rem(y, 2) == 0, y == r)

            @pl.when(jnp.logical_not(mine))
            def _():
                copy = pltpu.make_async_remote_copy(
                    src_ref=src.at[pl.ds(r * CHUNK, CHUNK), :],
                    dst_ref=dst.at[pl.ds(r * CHUNK, CHUNK), :],
                    send_sem=send.at[r],
                    recv_sem=recv.at[r],
                    device_id=device(y, zh, 1 - core, zl, x),
                    device_id_type=MESH,
                )
                if kind == 0:
                    copy.wait_recv()
                else:
                    copy.wait_send()


def add_rows(dst_at, parts, rows, step=64):
    @pl.loop(0, rows // step)
    def _(i):
        at = pl.multiple_of(i * step, step)
        total = parts[0](at, step).astype(F32)
        for part in parts[1:]:
            total = total + part(at, step).astype(F32)
        dst_at(at, step, total)


def gather_kernel(
    q_ref, k_ref, v_ref, gp_ref, w_ref,
    qz_ref, kv_ref, kt_ref, vt_ref, doz_ref,
    part, ra1, ra2, raz, tz, rbz, rb1, rb2, do_own,
    send, recv, qsend, qrecv, dsend, drecv,
):
    where = coords()
    y, zh, core, zl, x = where
    c = y * 4 + zh * 2 + core
    greet(*where)
    cp = Copies(send, recv)
    xr, xl = device(y, zh, core, zl, around(x + 1)), device(y, zh, core, zl, around(x - 1))
    zp = device(y, zh, core, 1 - zl, x)
    yr, yl = device(around(y + 1), zh, core, zl, x), device(around(y - 1), zh, core, zl, x)
    hp = device(y, 1 - zh, core, zl, x)
    mate = device(y, zh, 1 - core, zl, x)
    x_right, x_left, x_far = around(x + 1), around(x - 1), around(x + 2)
    y_right, y_left, y_far = around(y + 1), around(y - 1), around(y + 2)
    half_a, half_b = FIRST // 2, (ROWS - FIRST) // 2

    def slot(yy, zz, cc):
        return yy * 4 + zz * 2 + cc

    kv_ref[c, 0] = k_ref[...]
    kv_ref[c, 1] = v_ref[...]
    own = kv_ref.at[c]
    kv_z = cp.go(own, own, hp)
    kv_y0 = [cp.go(own, own, yr), cp.go(own, own, yl)]
    mates = [cp.go(own, own, mate)]
    deal_q = deal_out(q_ref, qz_ref, (qsend, qrecv), where)

    def compute(xx):
        @pl.loop(0, 2)
        def _(zz):
            rows = pl.ds(pl.multiple_of((zz * 4 + xx) * ROWS, ROWS), ROWS)
            part[xx, zz] = lax.dot_general(
                gp_ref[...], w_ref[rows, :], (((1,), (1,)), ((), ())), preferred_element_type=F32
            ).astype(BF)

    up_a, lo_a = pl.ds(0, half_a), pl.ds(half_a, half_a)
    all_b = pl.ds(FIRST, 2 * half_b)
    up_b, lo_b = pl.ds(FIRST, half_b), pl.ds(FIRST + half_b, half_b)
    compute(x_far)
    a1 = [
        cp.go(part.at[x_far, :, up_a, :], ra1.at[0], xr),
        cp.go(part.at[x_far, :, lo_a, :], ra1.at[1], xl),
    ]
    compute(x_right)
    a2 = [cp.go(part.at[x_right, :, lo_a, :], ra2.at[0, :, lo_a, :], xr)]
    compute(x_left)
    a2.append(cp.go(part.at[x_left, :, up_a, :], ra2.at[1, :, up_a, :], xl))
    compute(x)
    bz = cp.go(part.at[:, 1 - zl, all_b, :], rbz, zp)
    for r in range(4):
        deal_start(deal_q, r, where)
    deal_keep(q_ref, qz_ref, where)

    kv_z.wait_recv()
    other = kv_ref.at[slot(y, 1 - zh, core)]
    kv_y1 = [cp.go(other, other, yr), cp.go(other, other, yl)]
    mates.append(cp.go(other, other, mate))

    a1[0].wait_recv()
    for zz in range(2):
        def put(at, n, total, zz=zz):
            part[x_right, zz, pl.ds(at, n), :] = total.astype(BF)
        add_rows(put, [lambda at, n, zz=zz: part[x_right, zz, pl.ds(at, n), :], lambda at, n, zz=zz: ra1[0, zz, pl.ds(at, n), :]], half_a)
    a2.append(cp.go(part.at[x_right, :, up_a, :], ra2.at[0, :, up_a, :], xr))
    a1[1].wait_recv()
    for zz in range(2):
        def put(at, n, total, zz=zz):
            part[x_left, zz, pl.ds(half_a + at, n), :] = total.astype(BF)
        add_rows(put, [lambda at, n, zz=zz: part[x_left, zz, pl.ds(half_a + at, n), :], lambda at, n, zz=zz: ra1[1, zz, pl.ds(at, n), :]], half_a)
    a2.append(cp.go(part.at[x_left, :, lo_a, :], ra2.at[1, :, lo_a, :], xl))

    half_k = ROWS // 2
    early, late = pl.ds(0, half_k), pl.ds(half_k, half_k)

    def pass_on(got, zz):
        from_left, from_right = slot(y_left, zz, core), slot(y_right, zz, core)
        got[0].wait_recv()
        first = kv_ref.at[from_left, :, early, :]
        forwards = [cp.go(first, first, yr)]
        got[1].wait_recv()
        second = kv_ref.at[from_right, :, late, :]
        forwards.append(cp.go(second, second, yl))
        for s in (from_left, from_right):
            mates.append(cp.go(kv_ref.at[s], kv_ref.at[s], mate))
        return forwards

    far0 = pass_on(kv_y0, zh)

    bz.wait_recv()

    @pl.loop(0, 4)
    def _(xx):
        part[xx, zl, all_b, :] = (part[xx, zl, all_b, :].astype(F32) + rbz[xx].astype(F32)).astype(BF)

    b1 = [
        cp.go(part.at[x_far, zl, up_b, :], rb1.at[0], xr),
        cp.go(part.at[x_far, zl, lo_b, :], rb1.at[1], xl),
    ]
    b2 = [
        cp.go(part.at[x_right, zl, lo_b, :], rb2.at[0, pl.ds(half_b, half_b), :], xr),
        cp.go(part.at[x_left, zl, up_b, :], rb2.at[1, pl.ds(0, half_b), :], xl),
    ]
    far1 = pass_on(kv_y1, 1 - zh)
    b1[0].wait_recv()
    part[x_right, zl, up_b, :] = (part[x_right, zl, up_b, :].astype(F32) + rb1[0].astype(F32)).astype(BF)
    b2.append(cp.go(part.at[x_right, zl, up_b, :], rb2.at[0, pl.ds(0, half_b), :], xr))
    b1[1].wait_recv()
    part[x_left, zl, lo_b, :] = (part[x_left, zl, lo_b, :].astype(F32) + rb1[1].astype(F32)).astype(BF)
    b2.append(cp.go(part.at[x_left, zl, lo_b, :], rb2.at[1, pl.ds(half_b, half_b), :], xl))

    for copy in a2:
        copy.wait_recv()

    def put_away(at, n, total):
        tz[pl.ds(at, n), :] = total.astype(BF)

    def three(zz):
        return [
            lambda at, n: part[x, zz, pl.ds(at, n), :],
            lambda at, n: ra2[0, zz, pl.ds(at, n), :],
            lambda at, n: ra2[1, zz, pl.ds(at, n), :],
        ]

    add_rows(put_away, three(1 - zl), FIRST)
    az = cp.go(tz, raz, zp)

    for copies, zz in ((far0, zh), (far1, 1 - zh)):
        for copy in copies:
            copy.wait_recv()
        far = kv_ref.at[slot(y_far, zz, core)]
        mates.append(cp.go(far, far, mate))

    deal_do = deal_out(do_own, doz_ref, (dsend, drecv), where)
    for copy in b2:
        copy.wait_recv()

    def put_b(at, n, total):
        do_own[pl.ds(FIRST + at, n), :] = total.astype(BF)

    add_rows(
        put_b,
        [
            lambda at, n: part[x, zl, pl.ds(FIRST + at, n), :],
            lambda at, n: rb2[0, pl.ds(at, n), :],
            lambda at, n: rb2[1, pl.ds(at, n), :],
        ],
        ROWS - FIRST,
    )
    deal_start(deal_do, 3, where)

    def turn(s):
        cols = pl.ds(pl.multiple_of(s * ROWS, ROWS), ROWS)
        kt_ref[:, cols] = kv_ref[s, 0].T
        vt_ref[:, cols] = kv_ref[s, 1].T

    @pl.loop(0, 8)
    def _(i):
        turn(i * 2 + core)

    az.wait_recv()

    def put_a(at, n, total):
        do_own[pl.ds(at, n), :] = total.astype(BF)

    add_rows(put_a, three(zl) + [lambda at, n: raz[pl.ds(at, n), :]], FIRST)
    for r in range(3):
        deal_start(deal_do, r, where)
    deal_keep(do_own, doz_ref, where)

    for copy in mates:
        copy.wait_recv()

    @pl.loop(0, 8)
    def _(i):
        turn(i * 2 + 1 - core)

    deal_wait(q_ref, qz_ref, (qsend, qrecv), where)
    deal_wait(do_own, doz_ref, (dsend, drecv), where)
    cp.finish_sends()


def attend_kernel(
    len_ref, q_ref, do_ref, kv_ref, kt_ref, vt_ref,
    o_ref, dq_ref, dkv_ref,
    qt, qn, dot, don, ot, dqt, acc,
):
    y, zh, core, zl, x = coords()
    starts, run = [], jnp.int32(0)
    for d in range(len_ref.shape[0]):
        starts.append(run)
        run = run + len_ref[d]

    def start_of(pos):
        found = jnp.zeros_like(pos)
        for s in starts:
            found = jnp.maximum(found, jnp.where(s <= pos, s, 0))
        return found

    @pl.loop(0, CTX)
    def _(j):
        acc[j] = jnp.zeros(acc.shape[1:], F32)

    @pl.loop(0, 4)
    def _(slot):
        odd = lax.rem(slot, 2)
        piece = y + odd * (3 - 2 * y)
        seat = zh * 2 + core + odd * (1 - 2 * core)
        row0 = (slot * 16 + seat * 4 + piece) * CHUNK
        rows = pl.ds(pl.multiple_of(slot * CHUNK, CHUNK), CHUNK)
        for h in range(GROUP):
            cols = slice(h * HD, (h + 1) * HD)
            span = slice(h * CHUNK, (h + 1) * CHUNK)
            block = q_ref[rows, cols]
            qn[span, :] = block
            qt[:, span] = block.T
            block = do_ref[rows, cols]
            don[span, :] = block
            dot[:, span] = block.T
        pos = row0 + lax.rem(lax.broadcasted_iota(jnp.int32, (1, GROUP * CHUNK), 1), CHUNK)
        begin = start_of(pos)
        begin_first = start_of(row0)
        begin_last = start_of(row0 + CHUNK - 1)
        low = lax.div(begin_first, ROWS)
        high = lax.div(row0 + CHUNK - 1, ROWS) + 1

        def visible(j):
            key_pos = j * ROWS + lax.broadcasted_iota(jnp.int32, (ROWS, GROUP * CHUNK), 0)
            return jnp.logical_and(key_pos <= pos, key_pos >= begin)

        def whole(j):
            return jnp.logical_and(j * ROWS >= begin_last, (j + 1) * ROWS - 1 <= row0)

        ot[...] = jnp.zeros_like(ot)
        dqt[...] = jnp.zeros_like(dqt)

        def forward(j, carry):
            def step(masked, m, total):
                s = jnp.dot(kv_ref[j, 0], qt[...], preferred_element_type=F32)
                if masked:
                    seen = visible(j)
                    s = jnp.where(seen, s, LOWEST)
                m_new = jnp.maximum(m, jnp.max(s, axis=0, keepdims=True))
                p = jnp.exp2((s - m_new) * TO_LOG2)
                if masked:
                    p = jnp.where(seen, p, 0.0)
                scale = jnp.exp2((m - m_new) * TO_LOG2)
                total = total * scale + jnp.sum(p, axis=0, keepdims=True)
                cols = pl.ds(pl.multiple_of(j * ROWS, ROWS), ROWS)
                ot[...] = ot[...] * scale + jnp.dot(vt_ref[:, cols], p.astype(BF), preferred_element_type=F32)
                return m_new, total

            return lax.cond(whole(j), lambda a, b: step(False, a, b), lambda a, b: step(True, a, b), *carry)

        width = (1, GROUP * CHUNK)
        m, total = lax.fori_loop(low, high, forward, (jnp.full(width, LOWEST, F32), jnp.zeros(width, F32)))
        out = (ot[...] / total).astype(BF)
        delta = jnp.sum(out.astype(F32) * dot[...].astype(F32), axis=0, keepdims=True)
        log_total = m * TO_LOG2 + jnp.log2(total)
        for h in range(GROUP):
            o_ref[rows, slice(h * HD, (h + 1) * HD)] = out[:, h * CHUNK:(h + 1) * CHUNK].T

        def backward(j, carry):
            def step(masked):
                s = jnp.dot(kv_ref[j, 0], qt[...], preferred_element_type=F32)
                dp = jnp.dot(kv_ref[j, 1], dot[...], preferred_element_type=F32)
                if masked:
                    s = jnp.where(visible(j), s, LOWEST)
                p = jnp.exp2(s * TO_LOG2 - log_total)
                ds = (p * (dp - delta)).astype(BF)
                acc[j, 1] += jnp.dot(p.astype(BF), don[...], preferred_element_type=F32)
                acc[j, 0] += jnp.dot(ds, qn[...], preferred_element_type=F32)
                cols = pl.ds(pl.multiple_of(j * ROWS, ROWS), ROWS)
                dqt[...] += jnp.dot(kt_ref[:, cols], ds, preferred_element_type=F32)

            lax.cond(whole(j), lambda: step(False), lambda: step(True))
            return carry

        lax.fori_loop(low, high, backward, 0)
        grads = (dqt[...] * INV_ROOT).astype(BF)
        for h in range(GROUP):
            dq_ref[rows, slice(h * HD, (h + 1) * HD)] = grads[:, h * CHUNK:(h + 1) * CHUNK].T

    @pl.loop(0, CTX)
    def _(j):
        dkv_ref[j, 0] = (acc[j, 0] * INV_ROOT).astype(BF)
        dkv_ref[j, 1] = acc[j, 1].astype(BF)


def return_kernel(
    oz_ref, dqz_ref, dkv_ref, w_ref,
    pr_ref, dq_ref, dk_ref, dv_ref,
    every, total, projz, rc, dsum, r1, r2, tz, rz,
    send, recv, qsend, qrecv, psend, precv,
):
    where = coords()
    y, zh, core, zl, x = where
    greet(*where)
    cp = Copies(send, recv)
    xr, xl = device(y, zh, core, zl, around(x + 1)), device(y, zh, core, zl, around(x - 1))
    zp = device(y, zh, core, 1 - zl, x)
    yr, yl = device(around(y + 1), zh, core, zl, x), device(around(y - 1), zh, core, zl, x)
    hp = device(y, 1 - zh, core, zl, x)
    mate = device(y, zh, 1 - core, zl, x)
    x_right, x_left, x_far = around(x + 1), around(x - 1), around(x + 2)
    y_right, y_left, y_far = around(y + 1), around(y - 1), around(y + 2)
    half_a, half_b = FIRST // 2, (ROWS - FIRST) // 2
    all_a, all_b = pl.ds(0, FIRST), pl.ds(FIRST, 2 * half_b)
    up_a, lo_a = pl.ds(0, half_a), pl.ds(half_a, half_a)
    up_b, lo_b = pl.ds(FIRST, half_b), pl.ds(FIRST + half_b, half_b)

    def same(ref_at, dev):
        return cp.go(ref_at, ref_at, dev)

    core_swap = cp.go(dkv_ref.at[:, 1 - core], rc, mate)
    every[x, zl] = oz_ref[...]
    za = same(every.at[x, zl, all_a, :], zp)
    b0 = [same(every.at[x, zl, all_b, :], xr), same(every.at[x, zl, all_b, :], xl)]
    a0 = [same(every.at[x, zl, all_a, :], xr), same(every.at[x, zl, all_a, :], xl)]

    def deal_back(src, dst, sems, slot):
        yy, zz, cc, r = source_of(slot, y, zh, core)
        return pltpu.make_async_remote_copy(
            src_ref=src.at[pl.ds(slot * CHUNK, CHUNK), :],
            dst_ref=dst.at[pl.ds(r * CHUNK, CHUNK), :],
            send_sem=sems[0].at[slot],
            recv_sem=sems[1].at[r],
            device_id=device(yy, zz, cc, zl, x),
            device_id_type=MESH,
        )

    def start_back(src, dst, sems, slot):
        copy = deal_back(src, dst, sems, slot)
        if slot % 2:
            copy.start()
        else:
            @pl.when(y != slot)
            def _():
                copy.start()

    for s in range(4):
        start_back(dqz_ref, dq_ref, (qsend, qrecv), s)
    deal_keep(dqz_ref, dq_ref, where)

    def times(xx, zz, rows, n):
        at = pl.ds(pl.multiple_of((zz * 4 + xx) * ROWS, ROWS), ROWS)
        total[rows, :] += jnp.dot(every[xx, zz, rows, :], w_ref[at, :], preferred_element_type=F32)

    total[...] = jnp.zeros_like(total)
    times(x, zl, pl.ds(0, ROWS), ROWS)

    core_swap.wait_recv()

    @pl.loop(0, 8)
    def _(b):
        for kind in range(2):
            dsum[b, kind] = (dkv_ref[b, core, kind].astype(F32) + rc[b, kind].astype(F32)).astype(BF)

    half_k = ROWS // 2
    early, late = pl.ds(0, half_k), pl.ds(half_k, half_k)

    def pair(yy):
        return pl.ds(yy * 2, 2)

    d1 = [
        cp.go(dsum.at[pair(y_far), :, early, :], r1.at[0], yr),
        cp.go(dsum.at[pair(y_far), :, late, :], r1.at[1], yl),
    ]
    d2 = [
        cp.go(dsum.at[pair(y_right), :, late, :], r2.at[0, :, :, late, :], yr),
        cp.go(dsum.at[pair(y_left), :, early, :], r2.at[1, :, :, early, :], yl),
    ]

    za.wait_recv()
    a1 = [same(every.at[x, 1 - zl, all_a, :], xr), same(every.at[x, 1 - zl, all_a, :], xl)]
    times(x, 1 - zl, all_a, FIRST)

    b0[0].wait_recv()
    fb = [same(every.at[x_left, zl, up_b, :], xr)]
    b0[1].wait_recv()
    fb.append(same(every.at[x_right, zl, lo_b, :], xl))
    a0[0].wait_recv()
    fa0 = [same(every.at[x_left, zl, up_a, :], xr)]
    a0[1].wait_recv()
    fa0.append(same(every.at[x_right, zl, lo_a, :], xl))
    times(x_left, zl, pl.ds(0, ROWS), ROWS)
    times(x_right, zl, pl.ds(0, ROWS), ROWS)

    d1[0].wait_recv()

    def add_into(zz, kind, which, yy, rows):
        dsum[yy * 2 + zz, kind, rows, :] = (
            dsum[yy * 2 + zz, kind, rows, :].astype(F32) + r1[which, zz, kind].astype(F32)
        ).astype(BF)

    for zz in range(2):
        for kind in range(2):
            add_into(zz, kind, 0, y_right, early)
    d2.append(cp.go(dsum.at[pair(y_right), :, early, :], r2.at[0, :, :, early, :], yr))
    d1[1].wait_recv()
    for zz in range(2):
        for kind in range(2):
            add_into(zz, kind, 1, y_left, late)
    d2.append(cp.go(dsum.at[pair(y_left), :, late, :], r2.at[1, :, :, late, :], yl))

    for copy in fb:
        copy.wait_recv()
    zb = same(every.at[:, zl, all_b, :], zp)

    a1[0].wait_recv()
    fa1 = [same(every.at[x_left, 1 - zl, up_a, :], xr)]
    a1[1].wait_recv()
    fa1.append(same(every.at[x_right, 1 - zl, lo_a, :], xl))
    times(x_left, 1 - zl, all_a, FIRST)
    times(x_right, 1 - zl, all_a, FIRST)
    for copy in fa0:
        copy.wait_recv()
    times(x_far, zl, pl.ds(0, ROWS), ROWS)

    for copy in d2:
        copy.wait_recv()

    def three(zz, kind):
        return (
            dsum[y * 2 + zz, kind].astype(F32)
            + r2[0, zz, kind].astype(F32)
            + r2[1, zz, kind].astype(F32)
        )

    for kind in range(2):
        tz[kind] = three(1 - zh, kind).astype(BF)
    dz = cp.go(tz, rz, hp)

    for copy in fa1:
        copy.wait_recv()
    times(x_far, 1 - zl, all_a, FIRST)
    zb.wait_recv()

    @pl.loop(0, 4)
    def _(xx):
        times(xx, 1 - zl, all_b, ROWS - FIRST)

    projz[...] = total[...].astype(BF)
    for s in range(4):
        start_back(projz, pr_ref, (psend, precv), s)
    deal_keep(projz, pr_ref, where)

    dz.wait_recv()
    dk_ref[...] = (three(zh, 0) + rz[0].astype(F32)).astype(BF)
    dv_ref[...] = (three(zh, 1) + rz[1].astype(F32)).astype(BF)

    deal_wait(dqz_ref, dq_ref, (qsend, qrecv), where)
    deal_wait(projz, pr_ref, (psend, precv), where)
    cp.finish_sends()


def shape(*dims, dtype=BF):
    return jax.ShapeDtypeStruct(dims, dtype)


def params(collective=None):
    if collective is None:
        return pltpu.CompilerParams(vmem_limit_bytes=56 << 20)
    return pltpu.CompilerParams(
        collective_id=collective, has_side_effects=True, vmem_limit_bytes=56 << 20
    )


IN_VMEM = pl.BlockSpec(memory_space=pltpu.VMEM)
IN_SMEM = pl.BlockSpec(memory_space=pltpu.SMEM)
DMA = pltpu.SemaphoreType.DMA


def gather(queries, key_input, value_input, grad_projected, out_weight):
    half_a, half_b = FIRST // 2, (ROWS - FIRST) // 2
    return pl.pallas_call(
        gather_kernel,
        out_shape=(
            shape(ROWS, ROWS),
            shape(CTX, 2, ROWS, HD),
            shape(HD, TOKENS),
            shape(HD, TOKENS),
            shape(ROWS, ROWS),
        ),
        in_specs=[IN_VMEM] * 5,
        out_specs=(IN_VMEM,) * 5,
        scratch_shapes=[
            pltpu.VMEM((4, 2, ROWS, ROWS), BF),
            pltpu.VMEM((2, 2, half_a, ROWS), BF),
            pltpu.VMEM((2, 2, FIRST, ROWS), BF),
            pltpu.VMEM((FIRST, ROWS), BF),
            pltpu.VMEM((FIRST, ROWS), BF),
            pltpu.VMEM((4, ROWS - FIRST, ROWS), BF),
            pltpu.VMEM((2, half_b, ROWS), BF),
            pltpu.VMEM((2, ROWS - FIRST, ROWS), BF),
            pltpu.VMEM((ROWS, ROWS), BF),
            DMA((40,)), DMA((40,)),
            DMA((4,)), DMA((4,)), DMA((4,)), DMA((4,)),
        ],
        compiler_params=params(0),
        name="gather_inputs",
    )(queries, key_input, value_input, grad_projected, out_weight)


def attend(lengths, queries, grads, kv, keys_t, values_t):
    wide = GROUP * CHUNK
    return pl.pallas_call(
        attend_kernel,
        out_shape=(shape(ROWS, ROWS), shape(ROWS, ROWS), shape(CTX, 2, ROWS, HD)),
        in_specs=[IN_SMEM] + [IN_VMEM] * 5,
        out_specs=(IN_VMEM,) * 3,
        scratch_shapes=[
            pltpu.VMEM((HD, wide), BF),
            pltpu.VMEM((wide, HD), BF),
            pltpu.VMEM((HD, wide), BF),
            pltpu.VMEM((wide, HD), BF),
            pltpu.VMEM((HD, wide), F32),
            pltpu.VMEM((HD, wide), F32),
            pltpu.VMEM((CTX, 2, ROWS, HD), F32),
        ],
        compiler_params=params(),
        name="attend",
    )(lengths, queries, grads, kv, keys_t, values_t)


def give_back(attention, query_grads, kv_grads, out_weight):
    return pl.pallas_call(
        return_kernel,
        out_shape=(shape(ROWS, ROWS), shape(ROWS, ROWS), shape(ROWS, HD), shape(ROWS, HD)),
        in_specs=[IN_VMEM] * 4,
        out_specs=(IN_VMEM,) * 4,
        scratch_shapes=[
            pltpu.VMEM((4, 2, ROWS, ROWS), BF),
            pltpu.VMEM((ROWS, ROWS), F32),
            pltpu.VMEM((ROWS, ROWS), BF),
            pltpu.VMEM((8, 2, ROWS, HD), BF),
            pltpu.VMEM((8, 2, ROWS, HD), BF),
            pltpu.VMEM((2, 2, 2, ROWS // 2, HD), BF),
            pltpu.VMEM((2, 2, 2, ROWS, HD), BF),
            pltpu.VMEM((2, ROWS, HD), BF),
            pltpu.VMEM((2, ROWS, HD), BF),
            DMA((40,)), DMA((40,)),
            DMA((4,)), DMA((4,)), DMA((4,)), DMA((4,)),
        ],
        compiler_params=params(1),
        name="give_back",
    )(attention, query_grads, kv_grads.reshape(8, 2, 2, ROWS, HD), out_weight)


def body(queries, key_input, value_input, out_weight, lengths, grad_projected):
    qz, kv, keys_t, values_t, gz = gather(
        queries, key_input, value_input, grad_projected, out_weight
    )
    attention, dq, dkv = attend(lengths, qz, gz, kv, keys_t, values_t)
    return give_back(attention, dq, dkv, out_weight)


def solution(mesh):
    both = P("ctx", "head")
    return jax.shard_map(
        body,
        mesh=mesh,
        in_specs=(both, both, both, P(None, "head"), P(), both),
        out_specs=(both, both, both, both),
        check_vma=False,
    )
```

```python
import math

import jax
import jax.numpy as jnp
from jax import lax
from jax.experimental import pallas as pl
from jax.experimental.pallas import tpu as pltpu
from jax.sharding import PartitionSpec as P

HD = 128
GROUP = 4
ROWS = 512
CHUNK = 128
CTX = 16
TOKENS = 8192
INV_ROOT = 1.0 / math.sqrt(HD)
TO_LOG2 = INV_ROOT * math.log2(math.e)
LOWEST = -1e30
FLIP_Z = 0
FIRST = 384
MESH = pl.DeviceIdType.MESH
BF = jnp.bfloat16
F32 = jnp.float32


def coords():
    c = lax.axis_index("ctx")
    h = lax.axis_index("head")
    y = lax.div(c, 4)
    zh = lax.rem(lax.div(c, 2), 2)
    core = lax.rem(c, 2)
    zl = lax.div(h, 4)
    x = lax.rem(h, 4)
    return y, zh, core, zl, x


def device(y, zh, core, zl, x):
    return {"ctx": y * 4 + zh * 2 + core, "head": zl * 4 + x}


def around(i):
    return lax.rem(i + 4, 4)


def source_of(slot, y, zh, core):
    if slot % 2 == 0:
        return slot, zh, core, y
    return slot, zh + FLIP_Z * (1 - 2 * zh), 1 - core, 3 - y


class Copies:
    def __init__(self, send, recv):
        self.send, self.recv = send, recv
        self.made = []
        self.next = 0

    def new(self, src, dst, dev):
        i = self.next
        self.next += 1
        copy = pltpu.make_async_remote_copy(
            src_ref=src,
            dst_ref=dst,
            send_sem=self.send.at[i],
            recv_sem=self.recv.at[i],
            device_id=dev,
            device_id_type=MESH,
        )
        self.made.append(copy)
        return copy

    def go(self, src, dst, dev):
        copy = self.new(src, dst, dev)
        copy.start()
        return copy

    def finish_sends(self):
        for copy in self.made:
            copy.wait_send()


def greet(y, zh, core, zl, x):
    barrier = pltpu.get_barrier_semaphore()
    c = y * 4 + zh * 2 + core
    peers = [device(y, zh, core, zl, around(x + 1)), device(y, zh, core, zl, around(x - 1)), device(y, zh, core, 1 - zl, x)]
    for step in range(1, CTX):
        peers.append({"ctx": lax.rem(c + step, CTX), "head": zl * 4 + x})
    for peer in peers:
        pl.semaphore_signal(barrier, inc=1, device_id=peer, device_id_type=MESH)
    pl.semaphore_wait(barrier, len(peers))


def deal_out(src, dst, sems, where):
    y, zh, core, zl, x = where
    send, recv = sems
    odd = lax.rem(y, 2)
    copies = []
    for r in range(4):
        copy = pltpu.make_async_remote_copy(
            src_ref=src.at[pl.ds(r * CHUNK, CHUNK), :],
            dst_ref=dst.at[pl.ds(y * CHUNK, CHUNK), :],
            send_sem=send.at[r],
            recv_sem=recv.at[y],
            device_id=device(
                r + odd * (3 - 2 * r), zh + odd * FLIP_Z * (1 - 2 * zh), core + odd * (1 - 2 * core), zl, x
            ),
            device_id_type=MESH,
        )
        copies.append(copy)
    return copies


def deal_start(copies, r, where):
    y = where[0]
    mine = jnp.logical_and(lax.rem(y, 2) == 0, y == r)

    @pl.when(jnp.logical_not(mine))
    def _():
        copies[r].start()


def deal_keep(src, dst, where):
    y = where[0]

    @pl.when(lax.rem(y, 2) == 0)
    def _():
        rows = pl.ds(y * CHUNK, CHUNK)
        dst[rows, :] = src[rows, :]


def deal_wait(src, dst, sems, where):
    y, zh, core, zl, x = where
    send, recv = sems
    for r in range(4):
        for kind in (0, 1):
            mine = jnp.logical_and(lax.rem(y, 2) == 0, y == r)

            @pl.when(jnp.logical_not(mine))
            def _():
                copy = pltpu.make_async_remote_copy(
                    src_ref=src.at[pl.ds(r * CHUNK, CHUNK), :],
                    dst_ref=dst.at[pl.ds(r * CHUNK, CHUNK), :],
                    send_sem=send.at[r],
                    recv_sem=recv.at[r],
                    device_id=device(y, zh, 1 - core, zl, x),
                    device_id_type=MESH,
                )
                if kind == 0:
                    copy.wait_recv()
                else:
                    copy.wait_send()


def add_rows(dst_at, parts, rows, step=64):
    @pl.loop(0, rows // step)
    def _(i):
        at = pl.multiple_of(i * step, step)
        total = parts[0](at, step).astype(F32)
        for part in parts[1:]:
            total = total + part(at, step).astype(F32)
        dst_at(at, step, total)


def layer_kernel(
    len_ref, q_ref, k_ref, v_ref, gp_ref, w_ref,
    pr_ref, dq_ref, dk_ref, dv_ref,
    qz_ref, kv_ref, kt_ref, vt_ref, doz_ref, oz_ref, dqz_ref,
    part, ra1, ra2, raz, tz, rbz, rb1, rb2, do_own,
    qt, qn, dot, don, ot, outs, logs, deltas, dqt, acc,
    every, total, projz, dkv_out, rc, dsum, r1, r2, tzk, rz,
    send, recv, qsend, qrecv, dsend, drecv, gsend, grecv, psend, precv,
):
    where = coords()
    y, zh, core, zl, x = where
    c = y * 4 + zh * 2 + core
    greet(*where)
    cp = Copies(send, recv)
    xr, xl = device(y, zh, core, zl, around(x + 1)), device(y, zh, core, zl, around(x - 1))
    zp = device(y, zh, core, 1 - zl, x)
    yr, yl = device(around(y + 1), zh, core, zl, x), device(around(y - 1), zh, core, zl, x)
    hp = device(y, 1 - zh, core, zl, x)
    mate = device(y, zh, 1 - core, zl, x)
    x_right, x_left, x_far = around(x + 1), around(x - 1), around(x + 2)
    y_right, y_left, y_far = around(y + 1), around(y - 1), around(y + 2)
    half_a, half_b = FIRST // 2, (ROWS - FIRST) // 2

    def slot(yy, zz, cc):
        return yy * 4 + zz * 2 + cc

    kv_ref[c, 0] = k_ref[...]
    kv_ref[c, 1] = v_ref[...]
    own = kv_ref.at[c]
    kv_z = cp.go(own, own, hp)
    kv_y0 = [cp.go(own, own, yr), cp.go(own, own, yl)]
    mates = [cp.go(own, own, mate)]
    deal_q = deal_out(q_ref, qz_ref, (qsend, qrecv), where)

    for r in range(4):
        deal_start(deal_q, r, where)
    deal_keep(q_ref, qz_ref, where)

    def compute(xx):
        @pl.loop(0, 2)
        def _(zz):
            rows = pl.ds(pl.multiple_of((zz * 4 + xx) * ROWS, ROWS), ROWS)
            part[xx, zz] = lax.dot_general(
                gp_ref[...], w_ref[rows, :], (((1,), (1,)), ((), ())), preferred_element_type=F32
            ).astype(BF)

    up_a, lo_a = pl.ds(0, half_a), pl.ds(half_a, half_a)
    all_b = pl.ds(FIRST, 2 * half_b)
    up_b, lo_b = pl.ds(FIRST, half_b), pl.ds(FIRST + half_b, half_b)
    compute(x_far)
    a1 = [
        cp.go(part.at[x_far, :, up_a, :], ra1.at[0], xr),
        cp.go(part.at[x_far, :, lo_a, :], ra1.at[1], xl),
    ]
    compute(x_right)
    a2 = [cp.go(part.at[x_right, :, lo_a, :], ra2.at[0, :, lo_a, :], xr)]
    compute(x_left)
    a2.append(cp.go(part.at[x_left, :, up_a, :], ra2.at[1, :, up_a, :], xl))
    compute(x)
    bz = cp.go(part.at[:, 1 - zl, all_b, :], rbz, zp)

    kv_z.wait_recv()
    other = kv_ref.at[slot(y, 1 - zh, core)]
    kv_y1 = [cp.go(other, other, yr), cp.go(other, other, yl)]
    mates.append(cp.go(other, other, mate))

    a1[0].wait_recv()
    for zz in range(2):
        def put(at, n, total, zz=zz):
            part[x_right, zz, pl.ds(at, n), :] = total.astype(BF)
        add_rows(put, [lambda at, n, zz=zz: part[x_right, zz, pl.ds(at, n), :], lambda at, n, zz=zz: ra1[0, zz, pl.ds(at, n), :]], half_a)
    a2.append(cp.go(part.at[x_right, :, up_a, :], ra2.at[0, :, up_a, :], xr))
    a1[1].wait_recv()
    for zz in range(2):
        def put(at, n, total, zz=zz):
            part[x_left, zz, pl.ds(half_a + at, n), :] = total.astype(BF)
        add_rows(put, [lambda at, n, zz=zz: part[x_left, zz, pl.ds(half_a + at, n), :], lambda at, n, zz=zz: ra1[1, zz, pl.ds(at, n), :]], half_a)
    a2.append(cp.go(part.at[x_left, :, lo_a, :], ra2.at[1, :, lo_a, :], xl))

    half_k = ROWS // 2
    early, late = pl.ds(0, half_k), pl.ds(half_k, half_k)

    def pass_on(got, zz):
        from_left, from_right = slot(y_left, zz, core), slot(y_right, zz, core)
        got[0].wait_recv()
        first = kv_ref.at[from_left, :, early, :]
        forwards = [cp.go(first, first, yr)]
        got[1].wait_recv()
        second = kv_ref.at[from_right, :, late, :]
        forwards.append(cp.go(second, second, yl))
        for s in (from_left, from_right):
            mates.append(cp.go(kv_ref.at[s], kv_ref.at[s], mate))
        return forwards

    far0 = pass_on(kv_y0, zh)

    bz.wait_recv()

    @pl.loop(0, 4)
    def _(xx):
        part[xx, zl, all_b, :] = (part[xx, zl, all_b, :].astype(F32) + rbz[xx].astype(F32)).astype(BF)

    b1 = [
        cp.go(part.at[x_far, zl, up_b, :], rb1.at[0], xr),
        cp.go(part.at[x_far, zl, lo_b, :], rb1.at[1], xl),
    ]
    b2 = [
        cp.go(part.at[x_right, zl, lo_b, :], rb2.at[0, pl.ds(half_b, half_b), :], xr),
        cp.go(part.at[x_left, zl, up_b, :], rb2.at[1, pl.ds(0, half_b), :], xl),
    ]
    far1 = pass_on(kv_y1, 1 - zh)
    for copies, zz in ((far0, zh), (far1, 1 - zh)):
        for copy in copies:
            copy.wait_recv()
        far = kv_ref.at[slot(y_far, zz, core)]
        mates.append(cp.go(far, far, mate))

    def turn(s):
        cols = pl.ds(pl.multiple_of(s * ROWS, ROWS), ROWS)
        kt_ref[:, cols] = kv_ref[s, 0].T
        vt_ref[:, cols] = kv_ref[s, 1].T

    @pl.loop(0, 8)
    def _(i):
        turn(i * 2 + core)

    for copy in mates:
        copy.wait_recv()

    @pl.loop(0, 8)
    def _(i):
        turn(i * 2 + 1 - core)

    deal_wait(q_ref, qz_ref, (qsend, qrecv), where)

    starts, run = [], jnp.int32(0)
    for d in range(len_ref.shape[0]):
        starts.append(run)
        run = run + len_ref[d]
    wide = GROUP * CHUNK

    def place(slot):
        odd = lax.rem(slot, 2)
        piece = y + odd * (3 - 2 * y)
        seat = (zh + odd * FLIP_Z * (1 - 2 * zh)) * 2 + core + odd * (1 - 2 * core)
        return seat, (slot * 16 + seat * 4 + piece) * CHUNK

    def positions(slot):
        row0 = place(slot)[1]
        pos = row0 + lax.rem(lax.broadcasted_iota(jnp.int32, (1, wide), 1), CHUNK)
        begin = jnp.zeros_like(pos)
        for at in starts:
            begin = jnp.maximum(begin, jnp.where(at <= pos, at, 0))
        return pos, begin

    def masked_scores(j, slot, pos, begin):
        s = jnp.dot(kv_ref[j, 0], qt[slot], preferred_element_type=F32)
        key_pos = j * ROWS + lax.broadcasted_iota(jnp.int32, (ROWS, wide), 0)
        seen = jnp.logical_and(key_pos <= pos, key_pos >= begin)
        return jnp.where(seen, s, LOWEST)

    def columns(j):
        return pl.ds(pl.multiple_of(j * ROWS, ROWS), ROWS)

    def attend_slot(slot):
        rows = pl.ds(pl.multiple_of(slot * CHUNK, CHUNK), CHUNK)
        for h in range(GROUP):
            cols = slice(h * HD, (h + 1) * HD)
            span = slice(h * CHUNK, (h + 1) * CHUNK)
            block = qz_ref[rows, cols]
            qn[slot, span, :] = block
            qt[slot, :, span] = block.T
        pos, begin = positions(slot)
        ot[...] = jnp.zeros_like(ot)

        def step(blocks, m, total):
            ss = [masked_scores(j, slot, pos, begin) for j in blocks]
            m_new = m
            for s in ss:
                m_new = jnp.maximum(m_new, jnp.max(s, axis=0, keepdims=True))
            base = jnp.maximum(m_new, 0.5 * LOWEST)
            scale = jnp.exp2((m - base) * TO_LOG2)
            total = total * scale
            kept = ot[...] * scale
            for j, s in zip(blocks, ss):
                p = jnp.exp2((s - base) * TO_LOG2)
                total = total + jnp.sum(p, axis=0, keepdims=True)
                kept = kept + jnp.dot(vt_ref[:, columns(j)], p.astype(BF), preferred_element_type=F32)
            ot[...] = kept
            return m_new, total

        count = 4 * slot + place(slot)[0] + 1
        carry = (jnp.full((1, wide), LOWEST, F32), jnp.zeros((1, wide), F32))
        carry = lax.fori_loop(
            0, lax.div(count, 2), lambda i, c: step((2 * i, 2 * i + 1), *c), carry
        )
        m, total = lax.fori_loop(
            0, lax.rem(count, 2), lambda i, c: step((count - 1,), *c), carry
        )
        out = (ot[...] / total).astype(BF)
        outs[slot] = out
        logs[slot] = m * TO_LOG2 + jnp.log2(total)
        for h in range(GROUP):
            oz_ref[rows, slice(h * HD, (h + 1) * HD)] = out[:, h * CHUNK:(h + 1) * CHUNK].T

    @pl.loop(0, 2)
    def _(slot):
        attend_slot(slot)

    b1[0].wait_recv()
    part[x_right, zl, up_b, :] = (part[x_right, zl, up_b, :].astype(F32) + rb1[0].astype(F32)).astype(BF)
    b2.append(cp.go(part.at[x_right, zl, up_b, :], rb2.at[0, pl.ds(0, half_b), :], xr))
    b1[1].wait_recv()
    part[x_left, zl, lo_b, :] = (part[x_left, zl, lo_b, :].astype(F32) + rb1[1].astype(F32)).astype(BF)
    b2.append(cp.go(part.at[x_left, zl, lo_b, :], rb2.at[1, pl.ds(half_b, half_b), :], xl))

    attend_slot(jnp.int32(2))

    for copy in a2:
        copy.wait_recv()

    def put_away(at, n, total):
        tz[pl.ds(at, n), :] = total.astype(BF)

    def three(zz):
        return [
            lambda at, n: part[x, zz, pl.ds(at, n), :],
            lambda at, n: ra2[0, zz, pl.ds(at, n), :],
            lambda at, n: ra2[1, zz, pl.ds(at, n), :],
        ]

    add_rows(put_away, three(1 - zl), FIRST)
    az = cp.go(tz, raz, zp)

    attend_slot(jnp.int32(3))

    deal_do = deal_out(do_own, doz_ref, (dsend, drecv), where)
    for copy in b2:
        copy.wait_recv()

    def put_b(at, n, total):
        do_own[pl.ds(FIRST + at, n), :] = total.astype(BF)

    add_rows(
        put_b,
        [
            lambda at, n: part[x, zl, pl.ds(FIRST + at, n), :],
            lambda at, n: rb2[0, pl.ds(at, n), :],
            lambda at, n: rb2[1, pl.ds(at, n), :],
        ],
        ROWS - FIRST,
    )
    deal_start(deal_do, 3, where)

    all_a = pl.ds(0, FIRST)
    def same(ref_at, dev):
        return cp.go(ref_at, ref_at, dev)

    every[x, zl] = oz_ref[...]
    za = same(every.at[x, zl, all_a, :], zp)
    b0 = [same(every.at[x, zl, all_b, :], xr), same(every.at[x, zl, all_b, :], xl)]
    a0 = [same(every.at[x, zl, all_a, :], xr), same(every.at[x, zl, all_a, :], xl)]

    az.wait_recv()

    def put_a(at, n, total):
        do_own[pl.ds(at, n), :] = total.astype(BF)

    add_rows(put_a, three(zl) + [lambda at, n: raz[pl.ds(at, n), :]], FIRST)
    for r in range(3):
        deal_start(deal_do, r, where)
    deal_keep(do_own, doz_ref, where)

    def deal_back(src, dst, sems, slot):
        yy, zz, cc, r = source_of(slot, y, zh, core)
        return pltpu.make_async_remote_copy(
            src_ref=src.at[pl.ds(slot * CHUNK, CHUNK), :],
            dst_ref=dst.at[pl.ds(r * CHUNK, CHUNK), :],
            send_sem=sems[0].at[slot],
            recv_sem=sems[1].at[r],
            device_id=device(yy, zz, cc, zl, x),
            device_id_type=MESH,
        )

    def start_back(src, dst, sems, slot):
        copy = deal_back(src, dst, sems, slot)
        if slot % 2:
            copy.start()
        else:
            @pl.when(y != slot)
            def _():
                copy.start()

    def times(xx, zz, rows, n):
        at = pl.ds(pl.multiple_of((zz * 4 + xx) * ROWS, ROWS), ROWS)
        total[rows, :] += jnp.dot(every[xx, zz, rows, :], w_ref[at, :], preferred_element_type=F32)

    total[...] = jnp.zeros_like(total)
    times(x, zl, pl.ds(0, ROWS), ROWS)

    deal_wait(do_own, doz_ref, (dsend, drecv), where)

    @pl.loop(0, 4)
    def _(slot):
        rows = pl.ds(pl.multiple_of(slot * CHUNK, CHUNK), CHUNK)
        for h in range(GROUP):
            cols = slice(h * HD, (h + 1) * HD)
            span = slice(h * CHUNK, (h + 1) * CHUNK)
            block = doz_ref[rows, cols]
            don[slot, span, :] = block
            dot[slot, :, span] = block.T
        deltas[slot] = jnp.sum(outs[slot].astype(F32) * dot[slot].astype(F32), axis=0, keepdims=True)
        dqt[slot] = jnp.zeros(dqt.shape[1:], F32)

    @pl.loop(0, CTX)
    def _(j):
        acc[j] = jnp.zeros(acc.shape[1:], F32)

    half_k = ROWS // 2
    early, late = pl.ds(0, half_k), pl.ds(half_k, half_k)

    def sweep_quarter(yy):
        @pl.loop(yy, 4)
        def _(slot):
            pos, begin = positions(slot)
            log_total, delta = logs[slot], deltas[slot]

            def unit(j):
                s = masked_scores(j, slot, pos, begin)
                dp = jnp.dot(kv_ref[j, 1], dot[slot], preferred_element_type=F32)
                p = jnp.exp2(s * TO_LOG2 - log_total)
                ds = (p * (dp - delta)).astype(BF)
                acc[j, 1] += jnp.dot(p.astype(BF), don[slot], preferred_element_type=F32)
                acc[j, 0] += jnp.dot(ds, qn[slot], preferred_element_type=F32)
                dqt[slot] += jnp.dot(kt_ref[:, columns(j)], ds, preferred_element_type=F32)

            count = jnp.where(slot == yy, place(slot)[0] + 1, 4)

            @pl.loop(0, lax.div(count, 2))
            def _(i):
                unit(4 * yy + 2 * i)
                unit(4 * yy + 2 * i + 1)

            @pl.loop(0, lax.rem(count, 2))
            def _(i):
                unit(4 * yy + count - 1)

        @pl.loop(0, 2)
        def _(zz):
            j = yy * 4 + zz * 2 + 1 - core
            mine = yy * 2 + zz
            dkv_out[mine, 0] = (acc[j, 0] * INV_ROOT).astype(BF)
            dkv_out[mine, 1] = acc[j, 1].astype(BF)

        return cp.go(dkv_out.at[pair(yy)], rc.at[pair(yy)], mate)

    def pair(yy):
        return pl.ds(yy * 2, 2)

    def join(yy, swap):
        swap.wait_recv()

        @pl.loop(0, 2)
        def _(zz):
            j = yy * 4 + zz * 2 + core
            mine = yy * 2 + zz
            dsum[mine, 0] = (acc[j, 0] * INV_ROOT + rc[mine, 0].astype(F32)).astype(BF)
            dsum[mine, 1] = (acc[j, 1] + rc[mine, 1].astype(F32)).astype(BF)

    swap_far = sweep_quarter(y_far)
    za.wait_recv()
    a1 = [same(every.at[x, 1 - zl, all_a, :], xr), same(every.at[x, 1 - zl, all_a, :], xl)]
    b0[0].wait_recv()
    fb = [same(every.at[x_left, zl, up_b, :], xr)]
    b0[1].wait_recv()
    fb.append(same(every.at[x_right, zl, lo_b, :], xl))
    a0[0].wait_recv()
    fa0 = [same(every.at[x_left, zl, up_a, :], xr)]
    a0[1].wait_recv()
    fa0.append(same(every.at[x_right, zl, lo_a, :], xl))
    times(x, 1 - zl, all_a, FIRST)

    swap_right = sweep_quarter(y_right)
    join(y_far, swap_far)
    d1 = [
        cp.go(dsum.at[pair(y_far), :, early, :], r1.at[0], yr),
        cp.go(dsum.at[pair(y_far), :, late, :], r1.at[1], yl),
    ]
    a1[0].wait_recv()
    fa1 = [same(every.at[x_left, 1 - zl, up_a, :], xr)]
    a1[1].wait_recv()
    fa1.append(same(every.at[x_right, 1 - zl, lo_a, :], xl))
    times(x_left, zl, pl.ds(0, ROWS), ROWS)
    times(x_right, zl, pl.ds(0, ROWS), ROWS)

    swap_left = sweep_quarter(y_left)
    join(y_right, swap_right)
    d2 = [cp.go(dsum.at[pair(y_right), :, late, :], r2.at[0, :, :, late, :], yr)]
    for copy in fb:
        copy.wait_recv()
    zb = same(every.at[:, zl, all_b, :], zp)

    times(x_left, 1 - zl, all_a, FIRST)
    times(x_right, 1 - zl, all_a, FIRST)
    swap_own = sweep_quarter(y)

    @pl.loop(0, 4)
    def _(slot):
        rows = pl.ds(pl.multiple_of(slot * CHUNK, CHUNK), CHUNK)
        grads = (dqt[slot] * INV_ROOT).astype(BF)
        for h in range(GROUP):
            dqz_ref[rows, slice(h * HD, (h + 1) * HD)] = grads[:, h * CHUNK:(h + 1) * CHUNK].T

    join(y_left, swap_left)
    d2.append(cp.go(dsum.at[pair(y_left), :, early, :], r2.at[1, :, :, early, :], yl))
    for s in range(4):
        start_back(dqz_ref, dq_ref, (gsend, grecv), s)
    deal_keep(dqz_ref, dq_ref, where)

    d1[0].wait_recv()

    def add_into(zz, kind, which, yy, rows):
        dsum[yy * 2 + zz, kind, rows, :] = (
            dsum[yy * 2 + zz, kind, rows, :].astype(F32) + r1[which, zz, kind].astype(F32)
        ).astype(BF)

    for zz in range(2):
        for kind in range(2):
            add_into(zz, kind, 0, y_right, early)
    d2.append(cp.go(dsum.at[pair(y_right), :, early, :], r2.at[0, :, :, early, :], yr))
    d1[1].wait_recv()
    for zz in range(2):
        for kind in range(2):
            add_into(zz, kind, 1, y_left, late)
    d2.append(cp.go(dsum.at[pair(y_left), :, late, :], r2.at[1, :, :, late, :], yl))

    for copy in fa0:
        copy.wait_recv()
    times(x_far, zl, pl.ds(0, ROWS), ROWS)

    join(y, swap_own)
    for copy in d2:
        copy.wait_recv()

    def three(zz, kind):
        return (
            dsum[y * 2 + zz, kind].astype(F32)
            + r2[0, zz, kind].astype(F32)
            + r2[1, zz, kind].astype(F32)
        )

    for kind in range(2):
        tzk[kind] = three(1 - zh, kind).astype(BF)
    dz = cp.go(tzk, rz, hp)

    for copy in fa1:
        copy.wait_recv()
    times(x_far, 1 - zl, all_a, FIRST)
    zb.wait_recv()

    @pl.loop(0, 4)
    def _(xx):
        times(xx, 1 - zl, all_b, ROWS - FIRST)

    projz[...] = total[...].astype(BF)
    for s in range(4):
        start_back(projz, pr_ref, (psend, precv), s)
    deal_keep(projz, pr_ref, where)

    dz.wait_recv()
    dk_ref[...] = (three(zh, 0) + rz[0].astype(F32)).astype(BF)
    dv_ref[...] = (three(zh, 1) + rz[1].astype(F32)).astype(BF)

    deal_wait(dqz_ref, dq_ref, (gsend, grecv), where)
    deal_wait(projz, pr_ref, (psend, precv), where)
    cp.finish_sends()


def body(queries, key_input, value_input, out_weight, lengths, grad_projected):
    half_a, half_b = FIRST // 2, (ROWS - FIRST) // 2
    wide = GROUP * CHUNK
    rest = ROWS - FIRST

    def half(*dims):
        return pltpu.VMEM(dims, BF)

    def full(*dims):
        return pltpu.VMEM(dims, F32)

    def shape(*dims):
        return jax.ShapeDtypeStruct(dims, BF)

    in_vmem = pl.BlockSpec(memory_space=pltpu.VMEM)
    in_smem = pl.BlockSpec(memory_space=pltpu.SMEM)
    dma = pltpu.SemaphoreType.DMA
    return pl.pallas_call(
        layer_kernel,
        out_shape=(shape(ROWS, ROWS), shape(ROWS, ROWS), shape(ROWS, HD), shape(ROWS, HD)),
        in_specs=[in_smem] + [in_vmem] * 5,
        out_specs=(in_vmem,) * 4,
        scratch_shapes=[
            half(ROWS, ROWS), half(CTX, 2, ROWS, HD), half(HD, TOKENS), half(HD, TOKENS),
            half(ROWS, ROWS), half(ROWS, ROWS), half(ROWS, ROWS),
            half(4, 2, ROWS, ROWS), half(2, 2, half_a, ROWS), half(2, 2, FIRST, ROWS),
            half(FIRST, ROWS), half(FIRST, ROWS), half(4, rest, ROWS), half(2, half_b, ROWS),
            half(2, rest, ROWS), half(ROWS, ROWS),
            half(4, HD, wide), half(4, wide, HD), half(4, HD, wide), half(4, wide, HD),
            full(HD, wide), half(4, HD, wide), full(4, 1, wide), full(4, 1, wide),
            full(4, HD, wide), full(CTX, 2, ROWS, HD),
            half(4, 2, ROWS, ROWS), full(ROWS, ROWS), half(ROWS, ROWS),
            half(8, 2, ROWS, HD), half(8, 2, ROWS, HD), half(8, 2, ROWS, HD),
            half(2, 2, 2, ROWS // 2, HD), half(2, 2, 2, ROWS, HD), half(2, ROWS, HD), half(2, ROWS, HD),
            dma((80,)), dma((80,)),
        ] + [dma((4,))] * 8,
        compiler_params=pltpu.CompilerParams(
            collective_id=0, has_side_effects=True, vmem_limit_bytes=62 << 20
        ),
        name="layer",
    )(lengths, queries, key_input, value_input, grad_projected, out_weight)


def solution(mesh):
    both = P("ctx", "head")
    return jax.shard_map(
        body,
        mesh=mesh,
        in_specs=(both, both, both, P(None, "head"), P(), both),
        out_specs=(both, both, both, both),
        check_vma=False,
    )
```

```python
import math

import jax
import jax.numpy as jnp
from jax import lax
from jax.experimental import pallas as pl
from jax.experimental.pallas import tpu as pltpu
from jax.sharding import PartitionSpec as P

HD = 128
GROUP = 4
ROWS = 512
CHUNK = 128
CTX = 16
TOKENS = 8192
INV_ROOT = 1.0 / math.sqrt(HD)
TO_LOG2 = INV_ROOT * math.log2(math.e)
LOWEST = -1e30
FLIP_Z = 0
FIRST = 384
MESH = pl.DeviceIdType.MESH
BF = jnp.bfloat16
F32 = jnp.float32


def coords():
    c = lax.axis_index("ctx")
    h = lax.axis_index("head")
    y = lax.div(c, 4)
    zh = lax.rem(lax.div(c, 2), 2)
    core = lax.rem(c, 2)
    zl = lax.div(h, 4)
    x = lax.rem(h, 4)
    return y, zh, core, zl, x


def device(y, zh, core, zl, x):
    return {"ctx": y * 4 + zh * 2 + core, "head": zl * 4 + x}


def around(i):
    return lax.rem(i + 4, 4)


def source_of(slot, y, zh, core):
    if slot % 2 == 0:
        return slot, zh, core, y
    return slot, zh + FLIP_Z * (1 - 2 * zh), 1 - core, 3 - y


class Copies:
    def __init__(self, send, recv):
        self.send, self.recv = send, recv
        self.made = []
        self.next = 0

    def new(self, src, dst, dev):
        i = self.next
        self.next += 1
        copy = pltpu.make_async_remote_copy(
            src_ref=src,
            dst_ref=dst,
            send_sem=self.send.at[i],
            recv_sem=self.recv.at[i],
            device_id=dev,
            device_id_type=MESH,
        )
        self.made.append(copy)
        return copy

    def go(self, src, dst, dev):
        copy = self.new(src, dst, dev)
        copy.start()
        return copy

    def finish_sends(self):
        for copy in self.made:
            copy.wait_send()


def greet(y, zh, core, zl, x):
    barrier = pltpu.get_barrier_semaphore()
    c = y * 4 + zh * 2 + core
    peers = [device(y, zh, core, zl, around(x + 1)), device(y, zh, core, zl, around(x - 1)), device(y, zh, core, 1 - zl, x)]
    for step in range(1, CTX):
        peers.append({"ctx": lax.rem(c + step, CTX), "head": zl * 4 + x})
    for peer in peers:
        pl.semaphore_signal(barrier, inc=1, device_id=peer, device_id_type=MESH)
    pl.semaphore_wait(barrier, len(peers))


def deal_out(src, dst, sems, where):
    y, zh, core, zl, x = where
    send, recv = sems
    odd = lax.rem(y, 2)
    copies = []
    for r in range(4):
        copy = pltpu.make_async_remote_copy(
            src_ref=src.at[pl.ds(r * CHUNK, CHUNK), :],
            dst_ref=dst.at[pl.ds(y * CHUNK, CHUNK), :],
            send_sem=send.at[r],
            recv_sem=recv.at[y],
            device_id=device(
                r + odd * (3 - 2 * r), zh + odd * FLIP_Z * (1 - 2 * zh), core + odd * (1 - 2 * core), zl, x
            ),
            device_id_type=MESH,
        )
        copies.append(copy)
    return copies


def deal_start(copies, r, where):
    y = where[0]
    mine = jnp.logical_and(lax.rem(y, 2) == 0, y == r)

    @pl.when(jnp.logical_not(mine))
    def _():
        copies[r].start()


def deal_keep(src, dst, where):
    y = where[0]

    @pl.when(lax.rem(y, 2) == 0)
    def _():
        rows = pl.ds(y * CHUNK, CHUNK)
        dst[rows, :] = src[rows, :]


def deal_wait(src, dst, sems, where):
    y, zh, core, zl, x = where
    send, recv = sems
    for r in range(4):
        for kind in (0, 1):
            mine = jnp.logical_and(lax.rem(y, 2) == 0, y == r)

            @pl.when(jnp.logical_not(mine))
            def _():
                copy = pltpu.make_async_remote_copy(
                    src_ref=src.at[pl.ds(r * CHUNK, CHUNK), :],
                    dst_ref=dst.at[pl.ds(r * CHUNK, CHUNK), :],
                    send_sem=send.at[r],
                    recv_sem=recv.at[r],
                    device_id=device(y, zh, 1 - core, zl, x),
                    device_id_type=MESH,
                )
                if kind == 0:
                    copy.wait_recv()
                else:
                    copy.wait_send()


def add_rows(dst_at, parts, rows, step=64):
    @pl.loop(0, rows // step)
    def _(i):
        at = pl.multiple_of(i * step, step)
        total = parts[0](at, step).astype(F32)
        for part in parts[1:]:
            total = total + part(at, step).astype(F32)
        dst_at(at, step, total)


def layer_kernel(
    len_ref, q_ref, k_ref, v_ref, gp_ref, w_ref,
    pr_ref, dq_ref, dk_ref, dv_ref,
    qz_ref, kv_ref, kt_ref, vt_ref, doz_ref, oz_ref, dqz_ref,
    part, ra1, ra2, raz, tz, rbz, rb1, rb2, do_own,
    qt, qn, dot, don, ot, peaks, sums, outs, logs, deltas, dqt, acc,
    every, total, projz, dkv_out, rc, dsum, r1, r2, tzk, rz,
    send, recv, qsend, qrecv, dsend, drecv, gsend, grecv, psend, precv,
):
    where = coords()
    y, zh, core, zl, x = where
    c = y * 4 + zh * 2 + core
    greet(*where)
    cp = Copies(send, recv)
    xr, xl = device(y, zh, core, zl, around(x + 1)), device(y, zh, core, zl, around(x - 1))
    zp = device(y, zh, core, 1 - zl, x)
    yr, yl = device(around(y + 1), zh, core, zl, x), device(around(y - 1), zh, core, zl, x)
    hp = device(y, 1 - zh, core, zl, x)
    mate = device(y, zh, 1 - core, zl, x)
    x_right, x_left, x_far = around(x + 1), around(x - 1), around(x + 2)
    y_right, y_left, y_far = around(y + 1), around(y - 1), around(y + 2)
    half_a, half_b = FIRST // 2, (ROWS - FIRST) // 2

    def slot(yy, zz, cc):
        return yy * 4 + zz * 2 + cc

    kv_ref[c, 0] = k_ref[...]
    kv_ref[c, 1] = v_ref[...]
    own = kv_ref.at[c]
    kv_z = cp.go(own, own, hp)
    kv_y0 = [cp.go(own, own, yr), cp.go(own, own, yl)]
    mates = [cp.go(own, own, mate)]
    deal_q = deal_out(q_ref, qz_ref, (qsend, qrecv), where)

    for r in range(4):
        deal_start(deal_q, r, where)
    deal_keep(q_ref, qz_ref, where)

    def compute(xx):
        @pl.loop(0, 2)
        def _(zz):
            rows = pl.ds(pl.multiple_of((zz * 4 + xx) * ROWS, ROWS), ROWS)
            part[xx, zz] = lax.dot_general(
                gp_ref[...], w_ref[rows, :], (((1,), (1,)), ((), ())), preferred_element_type=F32
            ).astype(BF)

    up_a, lo_a = pl.ds(0, half_a), pl.ds(half_a, half_a)
    all_b = pl.ds(FIRST, 2 * half_b)
    up_b, lo_b = pl.ds(FIRST, half_b), pl.ds(FIRST + half_b, half_b)
    pieces = FIRST // CHUNK
    tops = [pl.ds(r * CHUNK, CHUNK // 2) for r in range(pieces)]
    lows = [pl.ds(r * CHUNK + CHUNK // 2, CHUNK // 2) for r in range(pieces)]
    fulls = [pl.ds(r * CHUNK, CHUNK) for r in range(pieces)]
    compute(x_far)
    a1 = [
        (
            cp.go(part.at[x_far, :, tops[r], :], ra1.at[0, r], xr),
            cp.go(part.at[x_far, :, lows[r], :], ra1.at[1, r], xl),
        )
        for r in range(pieces)
    ]
    compute(x_right)
    a2 = [[cp.go(part.at[x_right, :, lows[r], :], ra2.at[0, :, lows[r], :], xr)] for r in range(pieces)]
    compute(x_left)
    for r in range(pieces):
        a2[r].append(cp.go(part.at[x_left, :, tops[r], :], ra2.at[1, :, tops[r], :], xl))
    compute(x)
    bz = cp.go(part.at[:, 1 - zl, all_b, :], rbz, zp)

    kv_z.wait_recv()
    other = kv_ref.at[slot(y, 1 - zh, core)]
    kv_y1 = [cp.go(other, other, yr), cp.go(other, other, yl)]
    mates.append(cp.go(other, other, mate))

    half_k = ROWS // 2
    early, late = pl.ds(0, half_k), pl.ds(half_k, half_k)

    def pass_on(got, zz):
        from_left, from_right = slot(y_left, zz, core), slot(y_right, zz, core)
        got[0].wait_recv()
        first = kv_ref.at[from_left, :, early, :]
        forwards = [cp.go(first, first, yr)]
        got[1].wait_recv()
        second = kv_ref.at[from_right, :, late, :]
        forwards.append(cp.go(second, second, yl))
        swaps = [cp.go(kv_ref.at[s], kv_ref.at[s], mate) for s in (from_left, from_right)]
        return forwards, swaps

    def turn(s):
        cols = pl.ds(pl.multiple_of(s * ROWS, ROWS), ROWS)
        kt_ref[:, cols] = kv_ref[s, 0].T
        vt_ref[:, cols] = kv_ref[s, 1].T

    def turn_quarter(yy):
        @pl.loop(0, 4)
        def _(i):
            turn(yy * 4 + i)

    starts, run = [], jnp.int32(0)
    for d in range(len_ref.shape[0]):
        starts.append(run)
        run = run + len_ref[d]
    wide = GROUP * CHUNK

    def place(slot):
        odd = lax.rem(slot, 2)
        piece = y + odd * (3 - 2 * y)
        seat = (zh + odd * FLIP_Z * (1 - 2 * zh)) * 2 + core + odd * (1 - 2 * core)
        return seat, (slot * 16 + seat * 4 + piece) * CHUNK

    def positions(slot):
        row0 = place(slot)[1]
        pos = row0 + lax.rem(lax.broadcasted_iota(jnp.int32, (1, wide), 1), CHUNK)
        begin = jnp.zeros_like(pos)
        for at in starts:
            begin = jnp.maximum(begin, jnp.where(at <= pos, at, 0))
        return pos, begin

    def masked_scores(j, slot, pos, begin):
        s = jnp.dot(kv_ref[j, 0], qt[slot], preferred_element_type=F32)
        key_pos = j * ROWS + lax.broadcasted_iota(jnp.int32, (ROWS, wide), 0)
        seen = jnp.logical_and(key_pos <= pos, key_pos >= begin)
        return jnp.where(seen, s, LOWEST)

    def columns(j):
        return pl.ds(pl.multiple_of(j * ROWS, ROWS), ROWS)

    deal_wait(q_ref, qz_ref, (qsend, qrecv), where)

    @pl.loop(0, 4)
    def _(slot):
        rows = pl.ds(pl.multiple_of(slot * CHUNK, CHUNK), CHUNK)
        for h in range(GROUP):
            block = qz_ref[rows, slice(h * HD, (h + 1) * HD)]
            span = slice(h * CHUNK, (h + 1) * CHUNK)
            qn[slot, span, :] = block
            qt[slot, :, span] = block.T
        ot[slot] = jnp.zeros(ot.shape[1:], F32)
        peaks[slot] = jnp.full((1, wide), LOWEST, F32)
        sums[slot] = jnp.zeros((1, wide), F32)

    def units(slot, yy):
        return jnp.where(slot == yy, place(slot)[0] + 1, 4)

    def attend_quarter(yy):
        @pl.loop(yy, 4)
        def _(slot):
            pos, begin = positions(slot)

            def step(*blocks):
                ss = [masked_scores(j, slot, pos, begin) for j in blocks]
                m = peaks[slot]
                m_new = m
                for s in ss:
                    m_new = jnp.maximum(m_new, jnp.max(s, axis=0, keepdims=True))
                base = jnp.maximum(m_new, 0.5 * LOWEST)
                scale = jnp.exp2((m - base) * TO_LOG2)
                added = sums[slot] * scale
                kept = ot[slot] * scale
                for j, s in zip(blocks, ss):
                    p = jnp.exp2((s - base) * TO_LOG2)
                    added = added + jnp.sum(p, axis=0, keepdims=True)
                    kept = kept + jnp.dot(vt_ref[:, columns(j)], p.astype(BF), preferred_element_type=F32)
                ot[slot] = kept
                peaks[slot] = m_new
                sums[slot] = added

            count = units(slot, yy)

            @pl.loop(0, lax.div(count, 2))
            def _(i):
                step(4 * yy + 2 * i, 4 * yy + 2 * i + 1)

            @pl.loop(0, lax.rem(count, 2))
            def _(i):
                step(4 * yy + count - 1)

    def finish_slots():
        @pl.loop(0, 4)
        def _(slot):
            rows = pl.ds(pl.multiple_of(slot * CHUNK, CHUNK), CHUNK)
            out = (ot[slot] / sums[slot]).astype(BF)
            outs[slot] = out
            logs[slot] = peaks[slot] * TO_LOG2 + jnp.log2(sums[slot])
            for h in range(GROUP):
                oz_ref[rows, slice(h * HD, (h + 1) * HD)] = out[:, h * CHUNK:(h + 1) * CHUNK].T

    def pass_a1(r):
        for way, neighbour, spans, dev in ((0, x_right, tops, xr), (1, x_left, lows, xl)):
            a1[r][way].wait_recv()
            for zz in range(2):
                got = ra1[way, r, zz].astype(F32)
                part[neighbour, zz, spans[r], :] = (part[neighbour, zz, spans[r], :].astype(F32) + got).astype(BF)
            a2[r].append(cp.go(part.at[neighbour, :, spans[r], :], ra2.at[way, :, spans[r], :], dev))

    def three_a(zz, r):
        return (
            part[x, zz, fulls[r], :].astype(F32)
            + ra2[0, zz, fulls[r], :].astype(F32)
            + ra2[1, zz, fulls[r], :].astype(F32)
        )

    def sum_a(r):
        for copy in a2[r]:
            copy.wait_recv()
        tz[fulls[r], :] = three_a(1 - zl, r).astype(BF)
        return cp.go(tz.at[fulls[r], :], raz.at[fulls[r], :], zp)

    def end_a(r, az):
        az.wait_recv()
        do_own[fulls[r], :] = (three_a(zl, r) + raz[fulls[r], :].astype(F32)).astype(BF)
        deal_start(deal_do, r, where)

    for copy in mates:
        copy.wait_recv()
    turn_quarter(y)
    attend_quarter(y)
    pass_a1(0)
    far0, swaps0 = pass_on(kv_y0, zh)
    far1, swaps1 = pass_on(kv_y1, 1 - zh)
    for r in range(1, pieces):
        pass_a1(r)
    for copy in swaps0 + swaps1:
        copy.wait_recv()
    turn_quarter(y_right)
    turn_quarter(y_left)
    attend_quarter(y_right)
    bz.wait_recv()

    @pl.loop(0, 4)
    def _(xx):
        part[xx, zl, all_b, :] = (part[xx, zl, all_b, :].astype(F32) + rbz[xx].astype(F32)).astype(BF)

    b1 = [
        cp.go(part.at[x_far, zl, up_b, :], rb1.at[0], xr),
        cp.go(part.at[x_far, zl, lo_b, :], rb1.at[1], xl),
    ]
    b2 = [
        cp.go(part.at[x_right, zl, lo_b, :], rb2.at[0, pl.ds(half_b, half_b), :], xr),
        cp.go(part.at[x_left, zl, up_b, :], rb2.at[1, pl.ds(0, half_b), :], xl),
    ]
    last_swaps = []
    for copies, zz in ((far0, zh), (far1, 1 - zh)):
        for copy in copies:
            copy.wait_recv()
        far = kv_ref.at[slot(y_far, zz, core)]
        last_swaps.append(cp.go(far, far, mate))
    attend_quarter(y_left)
    b1[0].wait_recv()
    part[x_right, zl, up_b, :] = (part[x_right, zl, up_b, :].astype(F32) + rb1[0].astype(F32)).astype(BF)
    b2.append(cp.go(part.at[x_right, zl, up_b, :], rb2.at[0, pl.ds(0, half_b), :], xr))
    b1[1].wait_recv()
    part[x_left, zl, lo_b, :] = (part[x_left, zl, lo_b, :].astype(F32) + rb1[1].astype(F32)).astype(BF)
    b2.append(cp.go(part.at[x_left, zl, lo_b, :], rb2.at[1, pl.ds(half_b, half_b), :], xl))

    for copy in last_swaps:
        copy.wait_recv()
    turn_quarter(y_far)
    az = [sum_a(0)]
    attend_quarter(y_far)
    finish_slots()
    for r in range(1, pieces):
        az.append(sum_a(r))
    all_a = pl.ds(0, FIRST)

    def same(ref_at, dev):
        return cp.go(ref_at, ref_at, dev)

    every[x, zl] = oz_ref[...]
    za = same(every.at[x, zl, all_a, :], zp)
    b0 = [same(every.at[x, zl, all_b, :], xr), same(every.at[x, zl, all_b, :], xl)]
    a0 = [same(every.at[x, zl, all_a, :], xr), same(every.at[x, zl, all_a, :], xl)]

    deal_do = deal_out(do_own, doz_ref, (dsend, drecv), where)
    for r in range(pieces - 1):
        end_a(r, az[r])
    for copy in b2:
        copy.wait_recv()

    def put_b(at, n, total):
        do_own[pl.ds(FIRST + at, n), :] = total.astype(BF)

    add_rows(
        put_b,
        [
            lambda at, n: part[x, zl, pl.ds(FIRST + at, n), :],
            lambda at, n: rb2[0, pl.ds(at, n), :],
            lambda at, n: rb2[1, pl.ds(at, n), :],
        ],
        ROWS - FIRST,
    )
    deal_start(deal_do, 3, where)
    end_a(pieces - 1, az[pieces - 1])
    deal_keep(do_own, doz_ref, where)

    def deal_back(src, dst, sems, slot):
        yy, zz, cc, r = source_of(slot, y, zh, core)
        return pltpu.make_async_remote_copy(
            src_ref=src.at[pl.ds(slot * CHUNK, CHUNK), :],
            dst_ref=dst.at[pl.ds(r * CHUNK, CHUNK), :],
            send_sem=sems[0].at[slot],
            recv_sem=sems[1].at[r],
            device_id=device(yy, zz, cc, zl, x),
            device_id_type=MESH,
        )

    def start_back(src, dst, sems, slot):
        copy = deal_back(src, dst, sems, slot)
        if slot % 2:
            copy.start()
        else:
            @pl.when(y != slot)
            def _():
                copy.start()

    def times(xx, zz, rows, n):
        at = pl.ds(pl.multiple_of((zz * 4 + xx) * ROWS, ROWS), ROWS)
        total[rows, :] += jnp.dot(every[xx, zz, rows, :], w_ref[at, :], preferred_element_type=F32)

    total[...] = jnp.zeros_like(total)
    times(x, zl, pl.ds(0, ROWS), ROWS)

    deal_wait(do_own, doz_ref, (dsend, drecv), where)

    @pl.loop(0, 4)
    def _(slot):
        rows = pl.ds(pl.multiple_of(slot * CHUNK, CHUNK), CHUNK)
        for h in range(GROUP):
            cols = slice(h * HD, (h + 1) * HD)
            span = slice(h * CHUNK, (h + 1) * CHUNK)
            block = doz_ref[rows, cols]
            don[slot, span, :] = block
            dot[slot, :, span] = block.T
        deltas[slot] = jnp.sum(outs[slot].astype(F32) * dot[slot].astype(F32), axis=0, keepdims=True)
        dqt[slot] = jnp.zeros(dqt.shape[1:], F32)

    @pl.loop(0, CTX)
    def _(j):
        acc[j] = jnp.zeros(acc.shape[1:], F32)

    half_k = ROWS // 2
    early, late = pl.ds(0, half_k), pl.ds(half_k, half_k)

    def sweep_quarter(yy):
        @pl.loop(yy, 4)
        def _(slot):
            pos, begin = positions(slot)
            log_total, delta = logs[slot], deltas[slot]

            def unit(j):
                s = masked_scores(j, slot, pos, begin)
                dp = jnp.dot(kv_ref[j, 1], dot[slot], preferred_element_type=F32)
                p = jnp.exp2(s * TO_LOG2 - log_total)
                ds = (p * (dp - delta)).astype(BF)
                acc[j, 1] += jnp.dot(p.astype(BF), don[slot], preferred_element_type=F32)
                acc[j, 0] += jnp.dot(ds, qn[slot], preferred_element_type=F32)
                dqt[slot] += jnp.dot(kt_ref[:, columns(j)], ds, preferred_element_type=F32)

            count = units(slot, yy)

            @pl.loop(0, lax.div(count, 2))
            def _(i):
                unit(4 * yy + 2 * i)
                unit(4 * yy + 2 * i + 1)

            @pl.loop(0, lax.rem(count, 2))
            def _(i):
                unit(4 * yy + count - 1)

        @pl.loop(0, 2)
        def _(zz):
            j = yy * 4 + zz * 2 + 1 - core
            mine = yy * 2 + zz
            dkv_out[mine, 0] = (acc[j, 0] * INV_ROOT).astype(BF)
            dkv_out[mine, 1] = acc[j, 1].astype(BF)

        return cp.go(dkv_out.at[pair(yy)], rc.at[pair(yy)], mate)

    def pair(yy):
        return pl.ds(yy * 2, 2)

    def join(yy, swap):
        swap.wait_recv()

        @pl.loop(0, 2)
        def _(zz):
            j = yy * 4 + zz * 2 + core
            mine = yy * 2 + zz
            dsum[mine, 0] = (acc[j, 0] * INV_ROOT + rc[mine, 0].astype(F32)).astype(BF)
            dsum[mine, 1] = (acc[j, 1] + rc[mine, 1].astype(F32)).astype(BF)

    swap_far = sweep_quarter(y_far)
    za.wait_recv()
    a1 = [same(every.at[x, 1 - zl, all_a, :], xr), same(every.at[x, 1 - zl, all_a, :], xl)]
    b0[0].wait_recv()
    fb = [same(every.at[x_left, zl, up_b, :], xr)]
    b0[1].wait_recv()
    fb.append(same(every.at[x_right, zl, lo_b, :], xl))
    a0[0].wait_recv()
    fa0 = [same(every.at[x_left, zl, up_a, :], xr)]
    a0[1].wait_recv()
    fa0.append(same(every.at[x_right, zl, lo_a, :], xl))
    times(x, 1 - zl, all_a, FIRST)

    swap_right = sweep_quarter(y_right)
    join(y_far, swap_far)
    d1 = [
        cp.go(dsum.at[pair(y_far), :, early, :], r1.at[0], yr),
        cp.go(dsum.at[pair(y_far), :, late, :], r1.at[1], yl),
    ]
    a1[0].wait_recv()
    fa1 = [same(every.at[x_left, 1 - zl, up_a, :], xr)]
    a1[1].wait_recv()
    fa1.append(same(every.at[x_right, 1 - zl, lo_a, :], xl))
    times(x_left, zl, pl.ds(0, ROWS), ROWS)
    times(x_right, zl, pl.ds(0, ROWS), ROWS)

    swap_left = sweep_quarter(y_left)
    join(y_right, swap_right)
    d2 = [cp.go(dsum.at[pair(y_right), :, late, :], r2.at[0, :, :, late, :], yr)]
    for copy in fb:
        copy.wait_recv()
    zb = same(every.at[:, zl, all_b, :], zp)

    times(x_left, 1 - zl, all_a, FIRST)
    times(x_right, 1 - zl, all_a, FIRST)
    join(y_left, swap_left)
    d2.append(cp.go(dsum.at[pair(y_left), :, early, :], r2.at[1, :, :, early, :], yl))
    d1[0].wait_recv()

    def add_into(zz, kind, which, yy, rows):
        dsum[yy * 2 + zz, kind, rows, :] = (
            dsum[yy * 2 + zz, kind, rows, :].astype(F32) + r1[which, zz, kind].astype(F32)
        ).astype(BF)

    for zz in range(2):
        for kind in range(2):
            add_into(zz, kind, 0, y_right, early)
    d2.append(cp.go(dsum.at[pair(y_right), :, early, :], r2.at[0, :, :, early, :], yr))
    d1[1].wait_recv()
    for zz in range(2):
        for kind in range(2):
            add_into(zz, kind, 1, y_left, late)
    d2.append(cp.go(dsum.at[pair(y_left), :, late, :], r2.at[1, :, :, late, :], yl))

    swap_own = sweep_quarter(y)

    @pl.loop(0, 4)
    def _(slot):
        rows = pl.ds(pl.multiple_of(slot * CHUNK, CHUNK), CHUNK)
        grads = (dqt[slot] * INV_ROOT).astype(BF)
        for h in range(GROUP):
            dqz_ref[rows, slice(h * HD, (h + 1) * HD)] = grads[:, h * CHUNK:(h + 1) * CHUNK].T

    for s in range(4):
        start_back(dqz_ref, dq_ref, (gsend, grecv), s)
    deal_keep(dqz_ref, dq_ref, where)

    for copy in fa0:
        copy.wait_recv()
    times(x_far, zl, pl.ds(0, ROWS), ROWS)
    join(y, swap_own)
    for copy in d2:
        copy.wait_recv()

    def three(zz, kind):
        return (
            dsum[y * 2 + zz, kind].astype(F32)
            + r2[0, zz, kind].astype(F32)
            + r2[1, zz, kind].astype(F32)
        )

    for kind in range(2):
        tzk[kind] = three(1 - zh, kind).astype(BF)
    dz = cp.go(tzk, rz, hp)
    for copy in fa1:
        copy.wait_recv()
    times(x_far, 1 - zl, all_a, FIRST)
    projz[all_a, :] = total[all_a, :].astype(BF)
    for s in range(pieces):
        start_back(projz, pr_ref, (psend, precv), s)
    zb.wait_recv()

    @pl.loop(0, 4)
    def _(xx):
        times(xx, 1 - zl, all_b, ROWS - FIRST)

    projz[all_b, :] = total[all_b, :].astype(BF)
    for s in range(pieces, 4):
        start_back(projz, pr_ref, (psend, precv), s)
    deal_keep(projz, pr_ref, where)

    dz.wait_recv()
    dk_ref[...] = (three(zh, 0) + rz[0].astype(F32)).astype(BF)
    dv_ref[...] = (three(zh, 1) + rz[1].astype(F32)).astype(BF)

    deal_wait(dqz_ref, dq_ref, (gsend, grecv), where)
    deal_wait(projz, pr_ref, (psend, precv), where)
    cp.finish_sends()


def hand_over(*refs):
    sources, targets, done = refs[:4], refs[4:8], refs[8]
    copies = [pltpu.make_async_copy(a, b, done.at[i]) for i, (a, b) in enumerate(zip(sources, targets))]
    for copy in copies:
        copy.start()
    for copy in copies:
        copy.wait()


def body(queries, key_input, value_input, out_weight, lengths, grad_projected):
    half_b = (ROWS - FIRST) // 2
    wide = GROUP * CHUNK
    rest = ROWS - FIRST

    def half(*dims):
        return pltpu.VMEM(dims, BF)

    def full(*dims):
        return pltpu.VMEM(dims, F32)

    def shape(*dims):
        return jax.ShapeDtypeStruct(dims, BF)

    in_vmem = pl.BlockSpec(memory_space=pltpu.VMEM)
    in_smem = pl.BlockSpec(memory_space=pltpu.SMEM)
    dma = pltpu.SemaphoreType.DMA
    outputs = pl.pallas_call(
        layer_kernel,
        out_shape=(shape(ROWS, ROWS), shape(ROWS, ROWS), shape(ROWS, HD), shape(ROWS, HD)),
        in_specs=[in_smem] + [in_vmem] * 5,
        out_specs=(in_vmem,) * 4,
        scratch_shapes=[
            half(ROWS, ROWS), half(CTX, 2, ROWS, HD), half(HD, TOKENS), half(HD, TOKENS),
            half(ROWS, ROWS), half(ROWS, ROWS), half(ROWS, ROWS),
            half(4, 2, ROWS, ROWS), half(2, FIRST // CHUNK, 2, CHUNK // 2, ROWS), half(2, 2, FIRST, ROWS),
            half(FIRST, ROWS), half(FIRST, ROWS), half(4, rest, ROWS), half(2, half_b, ROWS),
            half(2, rest, ROWS), half(ROWS, ROWS),
            half(4, HD, wide), half(4, wide, HD), half(4, HD, wide), half(4, wide, HD),
            full(4, HD, wide), full(4, 1, wide), full(4, 1, wide), half(4, HD, wide), full(4, 1, wide), full(4, 1, wide),
            full(4, HD, wide), full(CTX, 2, ROWS, HD),
            half(4, 2, ROWS, ROWS), full(ROWS, ROWS), half(ROWS, ROWS),
            half(8, 2, ROWS, HD), half(8, 2, ROWS, HD), half(8, 2, ROWS, HD),
            half(2, 2, 2, ROWS // 2, HD), half(2, 2, 2, ROWS, HD), half(2, ROWS, HD), half(2, ROWS, HD),
            dma((96,)), dma((96,)),
        ] + [dma((4,))] * 8,
        compiler_params=pltpu.CompilerParams(
            collective_id=0, has_side_effects=True, vmem_limit_bytes=62 << 20
        ),
        name="layer",
    )(lengths, queries, key_input, value_input, grad_projected, out_weight)
    anywhere = pl.BlockSpec(memory_space=pl.ANY)
    return pl.pallas_call(
        hand_over,
        out_shape=(shape(ROWS, ROWS), shape(ROWS, ROWS), shape(ROWS, HD), shape(ROWS, HD)),
        in_specs=[anywhere] * 4,
        out_specs=(anywhere,) * 4,
        scratch_shapes=[dma((4,))],
        name="hand_over",
    )(*outputs)


def solution(mesh):
    both = P("ctx", "head")
    return jax.shard_map(
        body,
        mesh=mesh,
        in_specs=(both, both, both, P(None, "head"), P(), both),
        out_specs=(both, both, both, both),
        check_vma=False,
    )
```

```python
import math

import jax
import jax.numpy as jnp
from jax import lax
from jax.experimental import pallas as pl
from jax.experimental.pallas import tpu as pltpu
from jax.sharding import PartitionSpec as P

QH = 32
HD = 128
GROUP = 4
ROWS = 512
CHUNK = 128
CTX = 16
TOKENS = 8192
INV_ROOT = 1.0 / math.sqrt(HD)
TO_LOG2 = INV_ROOT * math.log2(math.e)
LOWEST = -1e30
FLIP_Z = 0
FIRST = 384
MESH = pl.DeviceIdType.MESH
BF = jnp.bfloat16
F32 = jnp.float32


def coords():
    c = lax.axis_index("ctx")
    h = lax.axis_index("head")
    y = lax.div(c, 4)
    zh = lax.rem(lax.div(c, 2), 2)
    core = lax.rem(c, 2)
    zl = lax.div(h, 4)
    x = lax.rem(h, 4)
    return y, zh, core, zl, x


def device(y, zh, core, zl, x):
    return {"ctx": y * 4 + zh * 2 + core, "head": zl * 4 + x}


def around(i):
    return lax.rem(i + 4, 4)


def source_of(slot, y, zh, core):
    if slot % 2 == 0:
        return slot, zh, core, y
    return slot, zh + FLIP_Z * (1 - 2 * zh), 1 - core, 3 - y


class Copies:
    def __init__(self, send, recv):
        self.send, self.recv = send, recv
        self.made = []
        self.next = 0

    def new(self, src, dst, dev):
        i = self.next
        self.next += 1
        copy = pltpu.make_async_remote_copy(
            src_ref=src,
            dst_ref=dst,
            send_sem=self.send.at[i],
            recv_sem=self.recv.at[i],
            device_id=dev,
            device_id_type=MESH,
        )
        self.made.append(copy)
        return copy

    def go(self, src, dst, dev):
        copy = self.new(src, dst, dev)
        copy.start()
        return copy

    def finish_sends(self):
        for copy in self.made:
            copy.wait_send()


def greet(y, zh, core, zl, x):
    barrier = pltpu.get_barrier_semaphore()
    c = y * 4 + zh * 2 + core
    peers = [device(y, zh, core, zl, around(x + 1)), device(y, zh, core, zl, around(x - 1)), device(y, zh, core, 1 - zl, x)]
    for step in range(1, CTX):
        peers.append({"ctx": lax.rem(c + step, CTX), "head": zl * 4 + x})
    for peer in peers:
        pl.semaphore_signal(barrier, inc=1, device_id=peer, device_id_type=MESH)
    pl.semaphore_wait(barrier, len(peers))


def deal_out(src, dst, sems, where):
    y, zh, core, zl, x = where
    send, recv = sems
    odd = lax.rem(y, 2)
    copies = []
    for r in range(4):
        copy = pltpu.make_async_remote_copy(
            src_ref=src.at[pl.ds(r * CHUNK, CHUNK), :],
            dst_ref=dst.at[pl.ds(y * CHUNK, CHUNK), :],
            send_sem=send.at[r],
            recv_sem=recv.at[y],
            device_id=device(
                r + odd * (3 - 2 * r), zh + odd * FLIP_Z * (1 - 2 * zh), core + odd * (1 - 2 * core), zl, x
            ),
            device_id_type=MESH,
        )
        copies.append(copy)
    return copies


def deal_start(copies, r, where):
    y = where[0]
    mine = jnp.logical_and(lax.rem(y, 2) == 0, y == r)

    @pl.when(jnp.logical_not(mine))
    def _():
        copies[r].start()


def deal_keep(src, dst, where):
    y = where[0]

    @pl.when(lax.rem(y, 2) == 0)
    def _():
        rows = pl.ds(y * CHUNK, CHUNK)
        dst[rows, :] = src[rows, :]


def deal_wait(src, dst, sems, where):
    y, zh, core, zl, x = where
    send, recv = sems
    for r in range(4):
        for kind in (0, 1):
            mine = jnp.logical_and(lax.rem(y, 2) == 0, y == r)

            @pl.when(jnp.logical_not(mine))
            def _():
                copy = pltpu.make_async_remote_copy(
                    src_ref=src.at[pl.ds(r * CHUNK, CHUNK), :],
                    dst_ref=dst.at[pl.ds(r * CHUNK, CHUNK), :],
                    send_sem=send.at[r],
                    recv_sem=recv.at[r],
                    device_id=device(y, zh, 1 - core, zl, x),
                    device_id_type=MESH,
                )
                if kind == 0:
                    copy.wait_recv()
                else:
                    copy.wait_send()


def add_rows(dst_at, parts, rows, step=64):
    @pl.loop(0, rows // step)
    def _(i):
        at = pl.multiple_of(i * step, step)
        total = parts[0](at, step).astype(F32)
        for part in parts[1:]:
            total = total + part(at, step).astype(F32)
        dst_at(at, step, total)


def layer_kernel(
    len_ref, q_ref, k_ref, v_ref, gp_ref, w_hbm,
    pr_ref, dq_ref, dk_ref, dv_ref,
    qz_ref, kv_ref, kt_ref, vt_ref, doz_ref, oz_ref, dqz_ref,
    part, ra1, ra2, raz, tz, rbz, rb1, rb2, do_own,
    qt, qn, dot, don, ot, peaks, sums, outs, logs, deltas, dqt, acc,
    every, total, projz, dkv_out, rc, dsum, r1, r2, tzk, rz,
    send, recv, qsend, qrecv, dsend, drecv, gsend, grecv, psend, precv, w_ref, wsem,
):
    where = coords()
    y, zh, core, zl, x = where
    c = y * 4 + zh * 2 + core
    weights = pltpu.make_async_copy(w_hbm, w_ref, wsem)
    weights.start()
    greet(*where)
    cp = Copies(send, recv)
    xr, xl = device(y, zh, core, zl, around(x + 1)), device(y, zh, core, zl, around(x - 1))
    zp = device(y, zh, core, 1 - zl, x)
    yr, yl = device(around(y + 1), zh, core, zl, x), device(around(y - 1), zh, core, zl, x)
    hp = device(y, 1 - zh, core, zl, x)
    mate = device(y, zh, 1 - core, zl, x)
    x_right, x_left, x_far = around(x + 1), around(x - 1), around(x + 2)
    y_right, y_left, y_far = around(y + 1), around(y - 1), around(y + 2)
    half_a, half_b = FIRST // 2, (ROWS - FIRST) // 2

    def slot(yy, zz, cc):
        return yy * 4 + zz * 2 + cc

    kv_ref[c, 0] = k_ref[...]
    kv_ref[c, 1] = v_ref[...]
    own = kv_ref.at[c]
    kv_z = cp.go(own, own, hp)
    kv_y0 = [cp.go(own, own, yr), cp.go(own, own, yl)]
    mates = [cp.go(own, own, mate)]
    deal_q = deal_out(q_ref, qz_ref, (qsend, qrecv), where)

    for r in range(4):
        deal_start(deal_q, r, where)
    deal_keep(q_ref, qz_ref, where)

    def compute(xx):
        @pl.loop(0, 2)
        def _(zz):
            rows = pl.ds(pl.multiple_of((zz * 4 + xx) * ROWS, ROWS), ROWS)
            part[xx, zz] = lax.dot_general(
                gp_ref[...], w_ref[rows, :], (((1,), (1,)), ((), ())), preferred_element_type=F32
            ).astype(BF)

    up_a, lo_a = pl.ds(0, half_a), pl.ds(half_a, half_a)
    all_b = pl.ds(FIRST, 2 * half_b)
    up_b, lo_b = pl.ds(FIRST, half_b), pl.ds(FIRST + half_b, half_b)
    pieces = FIRST // CHUNK
    tops = [pl.ds(r * CHUNK, CHUNK // 2) for r in range(pieces)]
    lows = [pl.ds(r * CHUNK + CHUNK // 2, CHUNK // 2) for r in range(pieces)]
    fulls = [pl.ds(r * CHUNK, CHUNK) for r in range(pieces)]
    weights.wait()
    compute(x_far)
    a1 = [
        (
            cp.go(part.at[x_far, :, tops[r], :], ra1.at[0, r], xr),
            cp.go(part.at[x_far, :, lows[r], :], ra1.at[1, r], xl),
        )
        for r in range(pieces)
    ]
    compute(x_right)
    a2 = [[cp.go(part.at[x_right, :, lows[r], :], ra2.at[0, :, lows[r], :], xr)] for r in range(pieces)]
    compute(x_left)
    for r in range(pieces):
        a2[r].append(cp.go(part.at[x_left, :, tops[r], :], ra2.at[1, :, tops[r], :], xl))
    compute(x)
    bz = cp.go(part.at[:, 1 - zl, all_b, :], rbz, zp)

    kv_z.wait_recv()
    other = kv_ref.at[slot(y, 1 - zh, core)]
    kv_y1 = [cp.go(other, other, yr), cp.go(other, other, yl)]
    mates.append(cp.go(other, other, mate))

    half_k = ROWS // 2
    early, late = pl.ds(0, half_k), pl.ds(half_k, half_k)

    def pass_on(got, zz):
        from_left, from_right = slot(y_left, zz, core), slot(y_right, zz, core)
        got[0].wait_recv()
        first = kv_ref.at[from_left, :, early, :]
        forwards = [cp.go(first, first, yr)]
        got[1].wait_recv()
        second = kv_ref.at[from_right, :, late, :]
        forwards.append(cp.go(second, second, yl))
        swaps = [cp.go(kv_ref.at[s], kv_ref.at[s], mate) for s in (from_left, from_right)]
        return forwards, swaps

    def turn(s):
        cols = pl.ds(pl.multiple_of(s * ROWS, ROWS), ROWS)
        kt_ref[:, cols] = kv_ref[s, 0].T
        vt_ref[:, cols] = kv_ref[s, 1].T

    def turn_quarter(yy):
        @pl.loop(0, 4)
        def _(i):
            turn(yy * 4 + i)

    starts, run = [], jnp.int32(0)
    for d in range(len_ref.shape[0]):
        starts.append(run)
        run = run + len_ref[d]
    wide = GROUP * CHUNK

    def place(slot):
        odd = lax.rem(slot, 2)
        piece = y + odd * (3 - 2 * y)
        seat = (zh + odd * FLIP_Z * (1 - 2 * zh)) * 2 + core + odd * (1 - 2 * core)
        return seat, (slot * 16 + seat * 4 + piece) * CHUNK

    def positions(slot):
        row0 = place(slot)[1]
        pos = row0 + lax.rem(lax.broadcasted_iota(jnp.int32, (1, wide), 1), CHUNK)
        begin = jnp.zeros_like(pos)
        for at in starts:
            begin = jnp.maximum(begin, jnp.where(at <= pos, at, 0))
        return pos, begin

    def masked_scores(j, slot, pos, begin, last):
        s = jnp.dot(kv_ref[j, 0], qt[slot], preferred_element_type=F32)
        key = lax.broadcasted_iota(jnp.int32, (ROWS, wide), 0)
        seen = key >= begin - j * ROWS
        if last:
            seen = jnp.logical_and(seen, key <= pos - j * ROWS)
        return jnp.where(seen, s, LOWEST)

    def columns(j):
        return pl.ds(pl.multiple_of(j * ROWS, ROWS), ROWS)

    def pass_a1(r):
        for way, neighbour, spans, dev in ((0, x_right, tops, xr), (1, x_left, lows, xl)):
            a1[r][way].wait_recv()
            for zz in range(2):
                got = ra1[way, r, zz].astype(F32)
                part[neighbour, zz, spans[r], :] = (part[neighbour, zz, spans[r], :].astype(F32) + got).astype(BF)
            a2[r].append(cp.go(part.at[neighbour, :, spans[r], :], ra2.at[way, :, spans[r], :], dev))

    def three_a(zz, r):
        return (
            part[x, zz, fulls[r], :].astype(F32)
            + ra2[0, zz, fulls[r], :].astype(F32)
            + ra2[1, zz, fulls[r], :].astype(F32)
        )

    def sum_a(r):
        for copy in a2[r]:
            copy.wait_recv()
        tz[fulls[r], :] = three_a(1 - zl, r).astype(BF)
        return cp.go(tz.at[fulls[r], :], raz.at[fulls[r], :], zp)

    def end_a(r, az):
        az.wait_recv()
        do_own[fulls[r], :] = (three_a(zl, r) + raz[fulls[r], :].astype(F32)).astype(BF)
        deal_start(deal_do, r, where)

    far0, swaps0 = pass_on(kv_y0, zh)
    for r in range(pieces - 1):
        pass_a1(r)
    deal_wait(q_ref, qz_ref, (qsend, qrecv), where)

    @pl.loop(0, 4)
    def _(slot):
        rows = pl.ds(pl.multiple_of(slot * CHUNK, CHUNK), CHUNK)
        for h in range(GROUP):
            block = qz_ref[rows, slice(h * HD, (h + 1) * HD)]
            span = slice(h * CHUNK, (h + 1) * CHUNK)
            qn[slot, span, :] = block
            qt[slot, :, span] = block.T
        ot[slot] = jnp.zeros(ot.shape[1:], F32)
        peaks[slot] = jnp.full((1, wide), LOWEST, F32)
        sums[slot] = jnp.zeros((1, wide), F32)

    def over_blocks(slot, yy, step):
        own = slot == yy
        count = jnp.where(own, place(slot)[0], 4)

        @pl.loop(0, lax.div(count, 2))
        def _(i):
            step(False, 4 * yy + 2 * i, 4 * yy + 2 * i + 1)

        @pl.loop(0, lax.rem(count, 2))
        def _(i):
            step(False, 4 * yy + count - 1)

        @pl.loop(0, jnp.where(own, 1, 0))
        def _(i):
            step(True, 4 * yy + count)

    def attend_quarter(yy):
        @pl.loop(yy, 4)
        def _(slot):
            pos, begin = positions(slot)

            def step(last, *blocks):
                ss = [masked_scores(j, slot, pos, begin, last) for j in blocks]
                m = peaks[slot]
                m_new = m
                for s in ss:
                    m_new = jnp.maximum(m_new, jnp.max(s, axis=0, keepdims=True))
                base = jnp.maximum(m_new, 0.5 * LOWEST)
                scale = jnp.exp2((m - base) * TO_LOG2)
                added = sums[slot] * scale
                kept = ot[slot] * scale
                for j, s in zip(blocks, ss):
                    p = jnp.exp2((s - base) * TO_LOG2)
                    added = added + jnp.sum(p, axis=0, keepdims=True)
                    kept = kept + jnp.dot(vt_ref[:, columns(j)], p.astype(BF), preferred_element_type=F32)
                ot[slot] = kept
                peaks[slot] = m_new
                sums[slot] = added

            over_blocks(slot, yy, step)

    def finish_slots():
        @pl.loop(0, 4)
        def _(slot):
            rows = pl.ds(pl.multiple_of(slot * CHUNK, CHUNK), CHUNK)
            out = (ot[slot] / sums[slot]).astype(BF)
            outs[slot] = out
            logs[slot] = peaks[slot] * TO_LOG2 + jnp.log2(sums[slot])
            for h in range(GROUP):
                oz_ref[rows, slice(h * HD, (h + 1) * HD)] = out[:, h * CHUNK:(h + 1) * CHUNK].T

    for copy in mates:
        copy.wait_recv()
    turn_quarter(y)
    pass_a1(pieces - 1)
    attend_quarter(y)
    far1, swaps1 = pass_on(kv_y1, 1 - zh)
    for copy in swaps0 + swaps1:
        copy.wait_recv()
    turn_quarter(y_right)
    turn_quarter(y_left)
    attend_quarter(y_right)
    bz.wait_recv()

    @pl.loop(0, 4)
    def _(xx):
        part[xx, zl, all_b, :] = (part[xx, zl, all_b, :].astype(F32) + rbz[xx].astype(F32)).astype(BF)

    b1 = [
        cp.go(part.at[x_far, zl, up_b, :], rb1.at[0], xr),
        cp.go(part.at[x_far, zl, lo_b, :], rb1.at[1], xl),
    ]
    b2 = [
        cp.go(part.at[x_right, zl, lo_b, :], rb2.at[0, pl.ds(half_b, half_b), :], xr),
        cp.go(part.at[x_left, zl, up_b, :], rb2.at[1, pl.ds(0, half_b), :], xl),
    ]
    last_swaps = []
    for copies, zz in ((far0, zh), (far1, 1 - zh)):
        for copy in copies:
            copy.wait_recv()
        far = kv_ref.at[slot(y_far, zz, core)]
        last_swaps.append(cp.go(far, far, mate))
    attend_quarter(y_left)
    b1[0].wait_recv()
    part[x_right, zl, up_b, :] = (part[x_right, zl, up_b, :].astype(F32) + rb1[0].astype(F32)).astype(BF)
    b2.append(cp.go(part.at[x_right, zl, up_b, :], rb2.at[0, pl.ds(0, half_b), :], xr))
    b1[1].wait_recv()
    part[x_left, zl, lo_b, :] = (part[x_left, zl, lo_b, :].astype(F32) + rb1[1].astype(F32)).astype(BF)
    b2.append(cp.go(part.at[x_left, zl, lo_b, :], rb2.at[1, pl.ds(half_b, half_b), :], xl))

    for copy in last_swaps:
        copy.wait_recv()
    turn_quarter(y_far)
    az = [sum_a(0)]
    attend_quarter(y_far)
    finish_slots()
    for r in range(1, pieces):
        az.append(sum_a(r))
    all_a = pl.ds(0, FIRST)

    def same(ref_at, dev):
        return cp.go(ref_at, ref_at, dev)

    every[x, zl] = oz_ref[...]
    za = same(every.at[x, zl, all_a, :], zp)
    b0 = [same(every.at[x, zl, all_b, :], xr), same(every.at[x, zl, all_b, :], xl)]
    a0 = [same(every.at[x, zl, all_a, :], xr), same(every.at[x, zl, all_a, :], xl)]

    deal_do = deal_out(do_own, doz_ref, (dsend, drecv), where)
    for r in range(pieces - 1):
        end_a(r, az[r])
    for copy in b2:
        copy.wait_recv()

    def put_b(at, n, total):
        do_own[pl.ds(FIRST + at, n), :] = total.astype(BF)

    add_rows(
        put_b,
        [
            lambda at, n: part[x, zl, pl.ds(FIRST + at, n), :],
            lambda at, n: rb2[0, pl.ds(at, n), :],
            lambda at, n: rb2[1, pl.ds(at, n), :],
        ],
        ROWS - FIRST,
    )
    deal_start(deal_do, 3, where)
    end_a(pieces - 1, az[pieces - 1])
    deal_keep(do_own, doz_ref, where)

    def deal_back(src, dst, sems, slot):
        yy, zz, cc, r = source_of(slot, y, zh, core)
        return pltpu.make_async_remote_copy(
            src_ref=src.at[pl.ds(slot * CHUNK, CHUNK), :],
            dst_ref=dst.at[pl.ds(r * CHUNK, CHUNK), :],
            send_sem=sems[0].at[slot],
            recv_sem=sems[1].at[r],
            device_id=device(yy, zz, cc, zl, x),
            device_id_type=MESH,
        )

    def start_back(src, dst, sems, slot):
        copy = deal_back(src, dst, sems, slot)
        if slot % 2:
            copy.start()
        else:
            @pl.when(y != slot)
            def _():
                copy.start()

    def times(xx, zz, rows, n):
        at = pl.ds(pl.multiple_of((zz * 4 + xx) * ROWS, ROWS), ROWS)
        total[rows, :] += jnp.dot(every[xx, zz, rows, :], w_ref[at, :], preferred_element_type=F32)

    total[...] = jnp.zeros_like(total)
    times(x, zl, pl.ds(0, ROWS), ROWS)

    deal_wait(do_own, doz_ref, (dsend, drecv), where)

    @pl.loop(0, 4)
    def _(slot):
        rows = pl.ds(pl.multiple_of(slot * CHUNK, CHUNK), CHUNK)
        for h in range(GROUP):
            cols = slice(h * HD, (h + 1) * HD)
            span = slice(h * CHUNK, (h + 1) * CHUNK)
            block = doz_ref[rows, cols]
            don[slot, span, :] = block
            dot[slot, :, span] = block.T
        deltas[slot] = jnp.sum(outs[slot].astype(F32) * dot[slot].astype(F32), axis=0, keepdims=True)
        dqt[slot] = jnp.zeros(dqt.shape[1:], F32)

    @pl.loop(0, CTX)
    def _(j):
        acc[j] = jnp.zeros(acc.shape[1:], F32)

    half_k = ROWS // 2
    early, late = pl.ds(0, half_k), pl.ds(half_k, half_k)

    def sweep_quarter(yy):
        @pl.loop(yy, 4)
        def _(slot):
            pos, begin = positions(slot)
            log_total, delta = logs[slot], deltas[slot]

            def unit(j, last):
                s = masked_scores(j, slot, pos, begin, last)
                dp = jnp.dot(kv_ref[j, 1], dot[slot], preferred_element_type=F32)
                p = jnp.exp2(s * TO_LOG2 - log_total)
                ds = (p * (dp - delta)).astype(BF)
                acc[j, 1] += jnp.dot(p.astype(BF), don[slot], preferred_element_type=F32)
                acc[j, 0] += jnp.dot(ds, qn[slot], preferred_element_type=F32)
                dqt[slot] += jnp.dot(kt_ref[:, columns(j)], ds, preferred_element_type=F32)

            def step(last, *blocks):
                for j in blocks:
                    unit(j, last)

            over_blocks(slot, yy, step)

        @pl.loop(0, 2)
        def _(zz):
            j = yy * 4 + zz * 2 + 1 - core
            mine = yy * 2 + zz
            dkv_out[mine, 0] = (acc[j, 0] * INV_ROOT).astype(BF)
            dkv_out[mine, 1] = acc[j, 1].astype(BF)

        return cp.go(dkv_out.at[pair(yy)], rc.at[pair(yy)], mate)

    def pair(yy):
        return pl.ds(yy * 2, 2)

    def join(yy, swap):
        swap.wait_recv()

        @pl.loop(0, 2)
        def _(zz):
            j = yy * 4 + zz * 2 + core
            mine = yy * 2 + zz
            dsum[mine, 0] = (acc[j, 0] * INV_ROOT + rc[mine, 0].astype(F32)).astype(BF)
            dsum[mine, 1] = (acc[j, 1] + rc[mine, 1].astype(F32)).astype(BF)

    za.wait_recv()
    a1 = [same(every.at[x, 1 - zl, all_a, :], xr), same(every.at[x, 1 - zl, all_a, :], xl)]
    b0[0].wait_recv()
    fb = [same(every.at[x_left, zl, up_b, :], xr)]
    b0[1].wait_recv()
    fb.append(same(every.at[x_right, zl, lo_b, :], xl))
    a0[0].wait_recv()
    fa0 = [same(every.at[x_left, zl, up_a, :], xr)]
    a0[1].wait_recv()
    fa0.append(same(every.at[x_right, zl, lo_a, :], xl))
    swap_far = sweep_quarter(y_far)
    times(x, 1 - zl, all_a, FIRST)

    swap_right = sweep_quarter(y_right)
    join(y_far, swap_far)
    d1 = [
        cp.go(dsum.at[pair(y_far), :, early, :], r1.at[0], yr),
        cp.go(dsum.at[pair(y_far), :, late, :], r1.at[1], yl),
    ]
    a1[0].wait_recv()
    fa1 = [same(every.at[x_left, 1 - zl, up_a, :], xr)]
    a1[1].wait_recv()
    fa1.append(same(every.at[x_right, 1 - zl, lo_a, :], xl))
    times(x_left, zl, pl.ds(0, ROWS), ROWS)
    times(x_right, zl, pl.ds(0, ROWS), ROWS)

    swap_left = sweep_quarter(y_left)
    join(y_right, swap_right)
    d2 = [cp.go(dsum.at[pair(y_right), :, late, :], r2.at[0, :, :, late, :], yr)]
    for copy in fb:
        copy.wait_recv()
    zb = same(every.at[:, zl, all_b, :], zp)

    times(x_left, 1 - zl, all_a, FIRST)
    times(x_right, 1 - zl, all_a, FIRST)
    join(y_left, swap_left)
    d2.append(cp.go(dsum.at[pair(y_left), :, early, :], r2.at[1, :, :, early, :], yl))
    d1[0].wait_recv()

    def add_into(zz, kind, which, yy, rows):
        dsum[yy * 2 + zz, kind, rows, :] = (
            dsum[yy * 2 + zz, kind, rows, :].astype(F32) + r1[which, zz, kind].astype(F32)
        ).astype(BF)

    for zz in range(2):
        for kind in range(2):
            add_into(zz, kind, 0, y_right, early)
    d2.append(cp.go(dsum.at[pair(y_right), :, early, :], r2.at[0, :, :, early, :], yr))
    d1[1].wait_recv()
    for zz in range(2):
        for kind in range(2):
            add_into(zz, kind, 1, y_left, late)
    d2.append(cp.go(dsum.at[pair(y_left), :, late, :], r2.at[1, :, :, late, :], yl))

    for copy in fa0:
        copy.wait_recv()
    times(x_far, zl, pl.ds(0, ROWS), ROWS)
    swap_own = sweep_quarter(y)

    @pl.loop(0, 4)
    def _(slot):
        rows = pl.ds(pl.multiple_of(slot * CHUNK, CHUNK), CHUNK)
        grads = (dqt[slot] * INV_ROOT).astype(BF)
        for h in range(GROUP):
            dqz_ref[rows, slice(h * HD, (h + 1) * HD)] = grads[:, h * CHUNK:(h + 1) * CHUNK].T

    for s in range(4):
        start_back(dqz_ref, dq_ref, (gsend, grecv), s)
    deal_keep(dqz_ref, dq_ref, where)

    join(y, swap_own)
    for copy in d2:
        copy.wait_recv()

    def three(zz, kind):
        return (
            dsum[y * 2 + zz, kind].astype(F32)
            + r2[0, zz, kind].astype(F32)
            + r2[1, zz, kind].astype(F32)
        )

    for kind in range(2):
        tzk[kind] = three(1 - zh, kind).astype(BF)
    dz = cp.go(tzk, rz, hp)
    for copy in fa1:
        copy.wait_recv()
    times(x_far, 1 - zl, all_a, FIRST)
    projz[all_a, :] = total[all_a, :].astype(BF)
    for s in range(pieces):
        start_back(projz, pr_ref, (psend, precv), s)
    zb.wait_recv()

    @pl.loop(0, 4)
    def _(xx):
        times(xx, 1 - zl, all_b, ROWS - FIRST)

    projz[all_b, :] = total[all_b, :].astype(BF)
    for s in range(pieces, 4):
        start_back(projz, pr_ref, (psend, precv), s)
    deal_keep(projz, pr_ref, where)

    dz.wait_recv()
    dk_ref[...] = (three(zh, 0) + rz[0].astype(F32)).astype(BF)
    dv_ref[...] = (three(zh, 1) + rz[1].astype(F32)).astype(BF)

    deal_wait(dqz_ref, dq_ref, (gsend, grecv), where)
    deal_wait(projz, pr_ref, (psend, precv), where)
    cp.finish_sends()


def hand_over(*refs):
    for source, target in zip(refs[:4], refs[4:]):
        target[...] = source[...]


def body(queries, key_input, value_input, out_weight, lengths, grad_projected):
    half_b = (ROWS - FIRST) // 2
    wide = GROUP * CHUNK
    rest = ROWS - FIRST

    def half(*dims):
        return pltpu.VMEM(dims, BF)

    def full(*dims):
        return pltpu.VMEM(dims, F32)

    def shape(*dims):
        return jax.ShapeDtypeStruct(dims, BF)

    in_vmem = pl.BlockSpec(memory_space=pltpu.VMEM)
    in_smem = pl.BlockSpec(memory_space=pltpu.SMEM)
    dma = pltpu.SemaphoreType.DMA
    outputs = pl.pallas_call(
        layer_kernel,
        out_shape=(shape(ROWS, ROWS), shape(ROWS, ROWS), shape(ROWS, HD), shape(ROWS, HD)),
        in_specs=[in_smem] + [in_vmem] * 4 + [pl.BlockSpec(memory_space=pl.ANY)],
        out_specs=(in_vmem,) * 4,
        scratch_shapes=[
            half(ROWS, ROWS), half(CTX, 2, ROWS, HD), half(HD, TOKENS), half(HD, TOKENS),
            half(ROWS, ROWS), half(ROWS, ROWS), half(ROWS, ROWS),
            half(4, 2, ROWS, ROWS), half(2, FIRST // CHUNK, 2, CHUNK // 2, ROWS), half(2, 2, FIRST, ROWS),
            half(FIRST, ROWS), half(FIRST, ROWS), half(4, rest, ROWS), half(2, half_b, ROWS),
            half(2, rest, ROWS), half(ROWS, ROWS),
            half(4, HD, wide), half(4, wide, HD), half(4, HD, wide), half(4, wide, HD),
            full(4, HD, wide), full(4, 1, wide), full(4, 1, wide), half(4, HD, wide), full(4, 1, wide), full(4, 1, wide),
            full(4, HD, wide), full(CTX, 2, ROWS, HD),
            half(4, 2, ROWS, ROWS), full(ROWS, ROWS), half(ROWS, ROWS),
            half(8, 2, ROWS, HD), half(8, 2, ROWS, HD), half(8, 2, ROWS, HD),
            half(2, 2, 2, ROWS // 2, HD), half(2, 2, 2, ROWS, HD), half(2, ROWS, HD), half(2, ROWS, HD),
            dma((96,)), dma((96,)),
        ] + [dma((4,))] * 8 + [half(QH * HD, ROWS), dma],
        compiler_params=pltpu.CompilerParams(
            collective_id=0, has_side_effects=True, vmem_limit_bytes=62 << 20
        ),
        name="layer",
    )(lengths, queries, key_input, value_input, grad_projected, out_weight)
    return pl.pallas_call(
        hand_over,
        out_shape=(shape(ROWS, ROWS), shape(ROWS, ROWS), shape(ROWS, HD), shape(ROWS, HD)),
        in_specs=[in_vmem] * 4,
        out_specs=(in_vmem,) * 4,
        name="hand_over",
    )(*outputs)


def solution(mesh):
    both = P("ctx", "head")
    return jax.shard_map(
        body,
        mesh=mesh,
        in_specs=(both, both, both, P(None, "head"), P(), both),
        out_specs=(both, both, both, both),
        check_vma=False,
    )
```

```python
import math

import jax
import jax.numpy as jnp
from jax import lax
from jax.experimental import pallas as pl
from jax.experimental.pallas import tpu as pltpu
from jax.sharding import PartitionSpec as P

QH = 32
HD = 128
GROUP = 4
ROWS = 512
CHUNK = 128
CTX = 16
TOKENS = 8192
INV_ROOT = 1.0 / math.sqrt(HD)
TO_LOG2 = INV_ROOT * math.log2(math.e)
LOWEST = -1e30
FLIP_Z = 0
FIRST = 384
MESH = pl.DeviceIdType.MESH
BF = jnp.bfloat16
F32 = jnp.float32


def coords():
    c = lax.axis_index("ctx")
    h = lax.axis_index("head")
    y = lax.div(c, 4)
    zh = lax.rem(lax.div(c, 2), 2)
    core = lax.rem(c, 2)
    zl = lax.div(h, 4)
    x = lax.rem(h, 4)
    return y, zh, core, zl, x


def device(y, zh, core, zl, x):
    return {"ctx": y * 4 + zh * 2 + core, "head": zl * 4 + x}


def around(i):
    return lax.rem(i + 4, 4)


def source_of(slot, y, zh, core):
    if slot % 2 == 0:
        return slot, zh, core, y
    return slot, zh + FLIP_Z * (1 - 2 * zh), 1 - core, 3 - y


class Copies:
    def __init__(self, send, recv):
        self.send, self.recv = send, recv
        self.made = []
        self.next = 0

    def new(self, src, dst, dev):
        i = self.next
        self.next += 1
        copy = pltpu.make_async_remote_copy(
            src_ref=src,
            dst_ref=dst,
            send_sem=self.send.at[i],
            recv_sem=self.recv.at[i],
            device_id=dev,
            device_id_type=MESH,
        )
        self.made.append(copy)
        return copy

    def go(self, src, dst, dev):
        copy = self.new(src, dst, dev)
        copy.start()
        return copy

    def finish_sends(self):
        for copy in self.made:
            copy.wait_send()


def greet(y, zh, core, zl, x):
    barrier = pltpu.get_barrier_semaphore()
    c = y * 4 + zh * 2 + core
    peers = [device(y, zh, core, zl, around(x + 1)), device(y, zh, core, zl, around(x - 1)), device(y, zh, core, 1 - zl, x)]
    for step in range(1, CTX):
        peers.append({"ctx": lax.rem(c + step, CTX), "head": zl * 4 + x})
    for peer in peers:
        pl.semaphore_signal(barrier, inc=1, device_id=peer, device_id_type=MESH)
    return lambda: pl.semaphore_wait(barrier, len(peers))


def deal_out(src, dst, sems, where):
    y, zh, core, zl, x = where
    send, recv = sems
    odd = lax.rem(y, 2)
    copies = []
    for r in range(4):
        copy = pltpu.make_async_remote_copy(
            src_ref=src.at[pl.ds(r * CHUNK, CHUNK), :],
            dst_ref=dst.at[pl.ds(y * CHUNK, CHUNK), :],
            send_sem=send.at[r],
            recv_sem=recv.at[y],
            device_id=device(
                r + odd * (3 - 2 * r), zh + odd * FLIP_Z * (1 - 2 * zh), core + odd * (1 - 2 * core), zl, x
            ),
            device_id_type=MESH,
        )
        copies.append(copy)
    return copies


def deal_start(copies, r, where):
    y = where[0]
    mine = jnp.logical_and(lax.rem(y, 2) == 0, y == r)

    @pl.when(jnp.logical_not(mine))
    def _():
        copies[r].start()


def deal_keep(src, dst, where):
    y = where[0]

    @pl.when(lax.rem(y, 2) == 0)
    def _():
        rows = pl.ds(y * CHUNK, CHUNK)
        dst[rows, :] = src[rows, :]


def deal_wait(src, dst, sems, where):
    y, zh, core, zl, x = where
    send, recv = sems
    for r in range(4):
        for kind in (0, 1):
            mine = jnp.logical_and(lax.rem(y, 2) == 0, y == r)

            @pl.when(jnp.logical_not(mine))
            def _():
                copy = pltpu.make_async_remote_copy(
                    src_ref=src.at[pl.ds(r * CHUNK, CHUNK), :],
                    dst_ref=dst.at[pl.ds(r * CHUNK, CHUNK), :],
                    send_sem=send.at[r],
                    recv_sem=recv.at[r],
                    device_id=device(y, zh, 1 - core, zl, x),
                    device_id_type=MESH,
                )
                if kind == 0:
                    copy.wait_recv()
                else:
                    copy.wait_send()


def add_rows(dst_at, parts, rows, step=64):
    @pl.loop(0, rows // step)
    def _(i):
        at = pl.multiple_of(i * step, step)
        total = parts[0](at, step).astype(F32)
        for part in parts[1:]:
            total = total + part(at, step).astype(F32)
        dst_at(at, step, total)


def layer_kernel(
    len_ref, q_ref, k_ref, v_ref, gp_ref, w_hbm,
    pr_ref, dq_ref, dk_ref, dv_ref,
    qz_ref, kv_ref, kt_ref, vt_ref, doz_ref, oz_ref, dqz_ref,
    part, ra1, ra2, raz, tz, rbz, rb1, rb2, do_own,
    qt, qn, dot, don, ot, peaks, sums, outs, logs, deltas, dqt, acc,
    every, total, projz, dkv_out, rc, dsum, r1, r2, tzk, rz,
    send, recv, qsend, qrecv, dsend, drecv, gsend, grecv, psend, precv, w_ref, wsem,
):
    where = coords()
    y, zh, core, zl, x = where
    c = y * 4 + zh * 2 + core
    weights = pltpu.make_async_copy(w_hbm, w_ref, wsem)
    weights.start()
    all_here = greet(*where)
    cp = Copies(send, recv)
    xr, xl = device(y, zh, core, zl, around(x + 1)), device(y, zh, core, zl, around(x - 1))
    zp = device(y, zh, core, 1 - zl, x)
    yr, yl = device(around(y + 1), zh, core, zl, x), device(around(y - 1), zh, core, zl, x)
    hp = device(y, 1 - zh, core, zl, x)
    mate = device(y, zh, 1 - core, zl, x)
    x_right, x_left, x_far = around(x + 1), around(x - 1), around(x + 2)
    y_right, y_left, y_far = around(y + 1), around(y - 1), around(y + 2)
    half_a, half_b = FIRST // 2, (ROWS - FIRST) // 2

    def slot(yy, zz, cc):
        return yy * 4 + zz * 2 + cc

    kv_ref[c, 0] = k_ref[...]
    kv_ref[c, 1] = v_ref[...]
    def compute(xx):
        @pl.loop(0, 2)
        def _(zz):
            rows = pl.ds(pl.multiple_of((zz * 4 + xx) * ROWS, ROWS), ROWS)
            part[xx, zz] = lax.dot_general(
                gp_ref[...], w_ref[rows, :], (((1,), (1,)), ((), ())), preferred_element_type=F32
            ).astype(BF)

    weights.wait()
    compute(x_far)
    all_here()
    own = kv_ref.at[c]
    kv_z = cp.go(own, own, hp)
    kv_y0 = [cp.go(own, own, yr), cp.go(own, own, yl)]
    mates = [cp.go(own, own, mate)]
    deal_q = deal_out(q_ref, qz_ref, (qsend, qrecv), where)
    for r in range(4):
        deal_start(deal_q, r, where)

    up_a, lo_a = pl.ds(0, half_a), pl.ds(half_a, half_a)
    all_b = pl.ds(FIRST, 2 * half_b)
    up_b, lo_b = pl.ds(FIRST, half_b), pl.ds(FIRST + half_b, half_b)
    pieces = FIRST // CHUNK
    tops = [pl.ds(r * CHUNK, CHUNK // 2) for r in range(pieces)]
    lows = [pl.ds(r * CHUNK + CHUNK // 2, CHUNK // 2) for r in range(pieces)]
    fulls = [pl.ds(r * CHUNK, CHUNK) for r in range(pieces)]
    a1 = [
        (
            cp.go(part.at[x_far, :, tops[r], :], ra1.at[0, r], xr),
            cp.go(part.at[x_far, :, lows[r], :], ra1.at[1, r], xl),
        )
        for r in range(pieces)
    ]
    compute(x_right)
    a2 = [[cp.go(part.at[x_right, :, lows[r], :], ra2.at[0, :, lows[r], :], xr)] for r in range(pieces)]
    compute(x_left)
    for r in range(pieces):
        a2[r].append(cp.go(part.at[x_left, :, tops[r], :], ra2.at[1, :, tops[r], :], xl))
    compute(x)
    deal_keep(q_ref, qz_ref, where)
    bz = cp.go(part.at[:, 1 - zl, all_b, :], rbz, zp)

    kv_z.wait_recv()
    other = kv_ref.at[slot(y, 1 - zh, core)]
    kv_y1 = [cp.go(other, other, yr), cp.go(other, other, yl)]
    mates.append(cp.go(other, other, mate))

    half_k = ROWS // 2
    early, late = pl.ds(0, half_k), pl.ds(half_k, half_k)

    def pass_on(got, zz):
        from_left, from_right = slot(y_left, zz, core), slot(y_right, zz, core)
        got[0].wait_recv()
        first = kv_ref.at[from_left, :, early, :]
        forwards = [cp.go(first, first, yr)]
        got[1].wait_recv()
        second = kv_ref.at[from_right, :, late, :]
        forwards.append(cp.go(second, second, yl))
        swaps = [cp.go(kv_ref.at[s], kv_ref.at[s], mate) for s in (from_left, from_right)]
        return forwards, swaps

    def turn(s):
        cols = pl.ds(pl.multiple_of(s * ROWS, ROWS), ROWS)
        kt_ref[:, cols] = kv_ref[s, 0].T
        vt_ref[:, cols] = kv_ref[s, 1].T

    def turn_quarter(yy):
        @pl.loop(0, 4)
        def _(i):
            turn(yy * 4 + i)

    starts, run = [], jnp.int32(0)
    for d in range(len_ref.shape[0]):
        starts.append(run)
        run = run + len_ref[d]
    wide = GROUP * CHUNK

    def place(slot):
        odd = lax.rem(slot, 2)
        piece = y + odd * (3 - 2 * y)
        seat = (zh + odd * FLIP_Z * (1 - 2 * zh)) * 2 + core + odd * (1 - 2 * core)
        return seat, (slot * 16 + seat * 4 + piece) * CHUNK

    def positions(slot):
        row0 = place(slot)[1]
        pos = row0 + lax.rem(lax.broadcasted_iota(jnp.int32, (1, wide), 1), CHUNK)
        begin = jnp.zeros_like(pos)
        for at in starts:
            begin = jnp.maximum(begin, jnp.where(at <= pos, at, 0))
        return pos, begin

    def masked_scores(j, slot, pos, begin, last):
        s = jnp.dot(kv_ref[j, 0], qt[slot], preferred_element_type=F32)
        key = lax.broadcasted_iota(jnp.int32, (ROWS, wide), 0)
        seen = key >= begin - j * ROWS
        if last:
            seen = jnp.logical_and(seen, key <= pos - j * ROWS)
        return jnp.where(seen, s, LOWEST)

    def columns(j):
        return pl.ds(pl.multiple_of(j * ROWS, ROWS), ROWS)

    def pass_a1(r):
        for way, neighbour, spans, dev in ((0, x_right, tops, xr), (1, x_left, lows, xl)):
            a1[r][way].wait_recv()
            for zz in range(2):
                got = ra1[way, r, zz].astype(F32)
                part[neighbour, zz, spans[r], :] = (part[neighbour, zz, spans[r], :].astype(F32) + got).astype(BF)
            a2[r].append(cp.go(part.at[neighbour, :, spans[r], :], ra2.at[way, :, spans[r], :], dev))

    def three_a(zz, r):
        return (
            part[x, zz, fulls[r], :].astype(F32)
            + ra2[0, zz, fulls[r], :].astype(F32)
            + ra2[1, zz, fulls[r], :].astype(F32)
        )

    def sum_a(r):
        for copy in a2[r]:
            copy.wait_recv()
        tz[fulls[r], :] = three_a(1 - zl, r).astype(BF)
        return cp.go(tz.at[fulls[r], :], raz.at[fulls[r], :], zp)

    def end_a(r, az):
        az.wait_recv()
        do_own[fulls[r], :] = (three_a(zl, r) + raz[fulls[r], :].astype(F32)).astype(BF)
        deal_start(deal_do, r, where)

    far0, swaps0 = pass_on(kv_y0, zh)
    for r in range(pieces - 1):
        pass_a1(r)
    deal_wait(q_ref, qz_ref, (qsend, qrecv), where)

    @pl.loop(0, 4)
    def _(slot):
        rows = pl.ds(pl.multiple_of(slot * CHUNK, CHUNK), CHUNK)
        for h in range(GROUP):
            block = qz_ref[rows, slice(h * HD, (h + 1) * HD)]
            span = slice(h * CHUNK, (h + 1) * CHUNK)
            qn[slot, span, :] = block
            qt[slot, :, span] = block.T
        ot[slot] = jnp.zeros(ot.shape[1:], F32)
        peaks[slot] = jnp.full((1, wide), LOWEST, F32)
        sums[slot] = jnp.zeros((1, wide), F32)

    def over_blocks(slot, yy, step):
        own = slot == yy
        count = jnp.where(own, place(slot)[0], 4)

        @pl.loop(0, lax.div(count, 2))
        def _(i):
            step(False, 4 * yy + 2 * i, 4 * yy + 2 * i + 1)

        @pl.loop(0, lax.rem(count, 2))
        def _(i):
            step(False, 4 * yy + count - 1)

        @pl.loop(0, jnp.where(own, 1, 0))
        def _(i):
            step(True, 4 * yy + count)

    def attend_quarter(yy):
        @pl.loop(yy, 4)
        def _(slot):
            pos, begin = positions(slot)

            def step(last, *blocks):
                ss = [masked_scores(j, slot, pos, begin, last) for j in blocks]
                m = peaks[slot]
                m_new = m
                for s in ss:
                    m_new = jnp.maximum(m_new, jnp.max(s, axis=0, keepdims=True))
                base = jnp.maximum(m_new, 0.5 * LOWEST)
                scale = jnp.exp2((m - base) * TO_LOG2)
                added = sums[slot] * scale
                kept = ot[slot] * scale
                for j, s in zip(blocks, ss):
                    p = jnp.exp2((s - base) * TO_LOG2)
                    added = added + jnp.sum(p, axis=0, keepdims=True)
                    kept = kept + jnp.dot(vt_ref[:, columns(j)], p.astype(BF), preferred_element_type=F32)
                ot[slot] = kept
                peaks[slot] = m_new
                sums[slot] = added

            over_blocks(slot, yy, step)

    def finish_slots():
        @pl.loop(0, 4)
        def _(slot):
            rows = pl.ds(pl.multiple_of(slot * CHUNK, CHUNK), CHUNK)
            out = (ot[slot] / sums[slot]).astype(BF)
            outs[slot] = out
            logs[slot] = peaks[slot] * TO_LOG2 + jnp.log2(sums[slot])
            for h in range(GROUP):
                oz_ref[rows, slice(h * HD, (h + 1) * HD)] = out[:, h * CHUNK:(h + 1) * CHUNK].T

    for copy in mates:
        copy.wait_recv()
    turn_quarter(y)
    pass_a1(pieces - 1)
    attend_quarter(y)
    far1, swaps1 = pass_on(kv_y1, 1 - zh)
    for copy in swaps0 + swaps1:
        copy.wait_recv()
    turn_quarter(y_right)
    turn_quarter(y_left)
    attend_quarter(y_right)
    bz.wait_recv()

    @pl.loop(0, 4)
    def _(xx):
        part[xx, zl, all_b, :] = (part[xx, zl, all_b, :].astype(F32) + rbz[xx].astype(F32)).astype(BF)

    b1 = [
        cp.go(part.at[x_far, zl, up_b, :], rb1.at[0], xr),
        cp.go(part.at[x_far, zl, lo_b, :], rb1.at[1], xl),
    ]
    b2 = [
        cp.go(part.at[x_right, zl, lo_b, :], rb2.at[0, pl.ds(half_b, half_b), :], xr),
        cp.go(part.at[x_left, zl, up_b, :], rb2.at[1, pl.ds(0, half_b), :], xl),
    ]
    attend_quarter(y_left)
    last_swaps = []
    for copies, zz in ((far0, zh), (far1, 1 - zh)):
        for copy in copies:
            copy.wait_recv()
        far = kv_ref.at[slot(y_far, zz, core)]
        last_swaps.append(cp.go(far, far, mate))
    b1[0].wait_recv()
    part[x_right, zl, up_b, :] = (part[x_right, zl, up_b, :].astype(F32) + rb1[0].astype(F32)).astype(BF)
    b2.append(cp.go(part.at[x_right, zl, up_b, :], rb2.at[0, pl.ds(0, half_b), :], xr))
    b1[1].wait_recv()
    part[x_left, zl, lo_b, :] = (part[x_left, zl, lo_b, :].astype(F32) + rb1[1].astype(F32)).astype(BF)
    b2.append(cp.go(part.at[x_left, zl, lo_b, :], rb2.at[1, pl.ds(half_b, half_b), :], xl))

    az = [sum_a(r) for r in range(pieces)]
    for copy in last_swaps:
        copy.wait_recv()
    turn_quarter(y_far)
    attend_quarter(y_far)
    finish_slots()
    all_a = pl.ds(0, FIRST)

    def same(ref_at, dev):
        return cp.go(ref_at, ref_at, dev)

    every[x, zl] = oz_ref[...]
    za = same(every.at[x, zl, all_a, :], zp)
    b0 = [same(every.at[x, zl, all_b, :], xr), same(every.at[x, zl, all_b, :], xl)]
    a0 = [same(every.at[x, zl, all_a, :], xr), same(every.at[x, zl, all_a, :], xl)]

    deal_do = deal_out(do_own, doz_ref, (dsend, drecv), where)
    for r in range(pieces - 1):
        end_a(r, az[r])
    for copy in b2:
        copy.wait_recv()

    def put_b(at, n, total):
        do_own[pl.ds(FIRST + at, n), :] = total.astype(BF)

    add_rows(
        put_b,
        [
            lambda at, n: part[x, zl, pl.ds(FIRST + at, n), :],
            lambda at, n: rb2[0, pl.ds(at, n), :],
            lambda at, n: rb2[1, pl.ds(at, n), :],
        ],
        ROWS - FIRST,
    )
    deal_start(deal_do, 3, where)
    end_a(pieces - 1, az[pieces - 1])
    deal_keep(do_own, doz_ref, where)

    def deal_back(src, dst, sems, slot):
        yy, zz, cc, r = source_of(slot, y, zh, core)
        return pltpu.make_async_remote_copy(
            src_ref=src.at[pl.ds(slot * CHUNK, CHUNK), :],
            dst_ref=dst.at[pl.ds(r * CHUNK, CHUNK), :],
            send_sem=sems[0].at[slot],
            recv_sem=sems[1].at[r],
            device_id=device(yy, zz, cc, zl, x),
            device_id_type=MESH,
        )

    def start_back(src, dst, sems, slot):
        copy = deal_back(src, dst, sems, slot)
        if slot % 2:
            copy.start()
        else:
            @pl.when(y != slot)
            def _():
                copy.start()

    def times(xx, zz, rows, n):
        at = pl.ds(pl.multiple_of((zz * 4 + xx) * ROWS, ROWS), ROWS)
        total[rows, :] += jnp.dot(every[xx, zz, rows, :], w_ref[at, :], preferred_element_type=F32)

    total[...] = jnp.zeros_like(total)
    times(x, zl, pl.ds(0, ROWS), ROWS)

    deal_wait(do_own, doz_ref, (dsend, drecv), where)

    @pl.loop(0, 4)
    def _(slot):
        rows = pl.ds(pl.multiple_of(slot * CHUNK, CHUNK), CHUNK)
        for h in range(GROUP):
            cols = slice(h * HD, (h + 1) * HD)
            span = slice(h * CHUNK, (h + 1) * CHUNK)
            block = doz_ref[rows, cols]
            don[slot, span, :] = block
            dot[slot, :, span] = block.T
        deltas[slot] = jnp.sum(outs[slot].astype(F32) * dot[slot].astype(F32), axis=0, keepdims=True)
        dqt[slot] = jnp.zeros(dqt.shape[1:], F32)

    @pl.loop(0, CTX)
    def _(j):
        acc[j] = jnp.zeros(acc.shape[1:], F32)

    half_k = ROWS // 2
    early, late = pl.ds(0, half_k), pl.ds(half_k, half_k)

    def sweep_quarter(yy):
        @pl.loop(yy, 4)
        def _(slot):
            pos, begin = positions(slot)
            log_total, delta = logs[slot], deltas[slot]

            def unit(j, last):
                s = masked_scores(j, slot, pos, begin, last)
                dp = jnp.dot(kv_ref[j, 1], dot[slot], preferred_element_type=F32)
                p = jnp.exp2(s * TO_LOG2 - log_total)
                ds = (p * (dp - delta)).astype(BF)
                acc[j, 1] += jnp.dot(p.astype(BF), don[slot], preferred_element_type=F32)
                acc[j, 0] += jnp.dot(ds, qn[slot], preferred_element_type=F32)
                dqt[slot] += jnp.dot(kt_ref[:, columns(j)], ds, preferred_element_type=F32)

            def step(last, *blocks):
                for j in blocks:
                    unit(j, last)

            over_blocks(slot, yy, step)

        @pl.loop(0, 2)
        def _(zz):
            j = yy * 4 + zz * 2 + 1 - core
            mine = yy * 2 + zz
            dkv_out[mine, 0] = (acc[j, 0] * INV_ROOT).astype(BF)
            dkv_out[mine, 1] = acc[j, 1].astype(BF)

        return cp.go(dkv_out.at[pair(yy)], rc.at[pair(yy)], mate)

    def pair(yy):
        return pl.ds(yy * 2, 2)

    def join(yy, swap):
        swap.wait_recv()

        @pl.loop(0, 2)
        def _(zz):
            j = yy * 4 + zz * 2 + core
            mine = yy * 2 + zz
            dsum[mine, 0] = (acc[j, 0] * INV_ROOT + rc[mine, 0].astype(F32)).astype(BF)
            dsum[mine, 1] = (acc[j, 1] + rc[mine, 1].astype(F32)).astype(BF)

    b0[0].wait_recv()
    fb = [same(every.at[x_left, zl, up_b, :], xr)]
    b0[1].wait_recv()
    fb.append(same(every.at[x_right, zl, lo_b, :], xl))
    za.wait_recv()
    a1 = [same(every.at[x, 1 - zl, all_a, :], xr), same(every.at[x, 1 - zl, all_a, :], xl)]
    a0[0].wait_recv()
    fa0 = [same(every.at[x_left, zl, up_a, :], xr)]
    a0[1].wait_recv()
    fa0.append(same(every.at[x_right, zl, lo_a, :], xl))
    swap_far = sweep_quarter(y_far)
    for copy in fb:
        copy.wait_recv()
    zb = same(every.at[:, zl, all_b, :], zp)
    times(x, 1 - zl, all_a, FIRST)

    join(y_far, swap_far)
    d1 = [
        cp.go(dsum.at[pair(y_far), :, early, :], r1.at[0], yr),
        cp.go(dsum.at[pair(y_far), :, late, :], r1.at[1], yl),
    ]

    swap_right = sweep_quarter(y_right)
    a1[0].wait_recv()
    fa1 = [same(every.at[x_left, 1 - zl, up_a, :], xr)]
    a1[1].wait_recv()
    fa1.append(same(every.at[x_right, 1 - zl, lo_a, :], xl))
    times(x_left, zl, pl.ds(0, ROWS), ROWS)
    times(x_right, zl, pl.ds(0, ROWS), ROWS)

    swap_left = sweep_quarter(y_left)
    join(y_right, swap_right)
    d2 = [cp.go(dsum.at[pair(y_right), :, late, :], r2.at[0, :, :, late, :], yr)]

    times(x_left, 1 - zl, all_a, FIRST)
    times(x_right, 1 - zl, all_a, FIRST)
    join(y_left, swap_left)
    d2.append(cp.go(dsum.at[pair(y_left), :, early, :], r2.at[1, :, :, early, :], yl))
    d1[0].wait_recv()

    def add_into(zz, kind, which, yy, rows):
        dsum[yy * 2 + zz, kind, rows, :] = (
            dsum[yy * 2 + zz, kind, rows, :].astype(F32) + r1[which, zz, kind].astype(F32)
        ).astype(BF)

    for zz in range(2):
        for kind in range(2):
            add_into(zz, kind, 0, y_right, early)
    d2.append(cp.go(dsum.at[pair(y_right), :, early, :], r2.at[0, :, :, early, :], yr))
    d1[1].wait_recv()
    for zz in range(2):
        for kind in range(2):
            add_into(zz, kind, 1, y_left, late)
    d2.append(cp.go(dsum.at[pair(y_left), :, late, :], r2.at[1, :, :, late, :], yl))

    for copy in fa0:
        copy.wait_recv()
    times(x_far, zl, pl.ds(0, ROWS), ROWS)
    swap_own = sweep_quarter(y)

    @pl.loop(0, 4)
    def _(slot):
        rows = pl.ds(pl.multiple_of(slot * CHUNK, CHUNK), CHUNK)
        grads = (dqt[slot] * INV_ROOT).astype(BF)
        for h in range(GROUP):
            dqz_ref[rows, slice(h * HD, (h + 1) * HD)] = grads[:, h * CHUNK:(h + 1) * CHUNK].T

    for s in range(4):
        start_back(dqz_ref, dq_ref, (gsend, grecv), s)
    deal_keep(dqz_ref, dq_ref, where)

    join(y, swap_own)
    for copy in d2:
        copy.wait_recv()

    def three(zz, kind):
        return (
            dsum[y * 2 + zz, kind].astype(F32)
            + r2[0, zz, kind].astype(F32)
            + r2[1, zz, kind].astype(F32)
        )

    for kind in range(2):
        tzk[kind] = three(1 - zh, kind).astype(BF)
    dz = cp.go(tzk, rz, hp)
    for copy in fa1:
        copy.wait_recv()
    times(x_far, 1 - zl, all_a, FIRST)
    projz[all_a, :] = total[all_a, :].astype(BF)
    for s in range(pieces):
        start_back(projz, pr_ref, (psend, precv), s)
    zb.wait_recv()

    @pl.loop(0, 4)
    def _(xx):
        times(xx, 1 - zl, all_b, ROWS - FIRST)

    projz[all_b, :] = total[all_b, :].astype(BF)
    for s in range(pieces, 4):
        start_back(projz, pr_ref, (psend, precv), s)
    deal_keep(projz, pr_ref, where)

    dz.wait_recv()
    dk_ref[...] = (three(zh, 0) + rz[0].astype(F32)).astype(BF)
    dv_ref[...] = (three(zh, 1) + rz[1].astype(F32)).astype(BF)

    deal_wait(dqz_ref, dq_ref, (gsend, grecv), where)
    deal_wait(projz, pr_ref, (psend, precv), where)
    cp.finish_sends()


def hand_over(*refs):
    for source, target in zip(refs[:4], refs[4:]):
        target[...] = source[...]


def body(queries, key_input, value_input, out_weight, lengths, grad_projected):
    half_b = (ROWS - FIRST) // 2
    wide = GROUP * CHUNK
    rest = ROWS - FIRST

    def half(*dims):
        return pltpu.VMEM(dims, BF)

    def full(*dims):
        return pltpu.VMEM(dims, F32)

    def shape(*dims):
        return jax.ShapeDtypeStruct(dims, BF)

    in_vmem = pl.BlockSpec(memory_space=pltpu.VMEM)
    in_smem = pl.BlockSpec(memory_space=pltpu.SMEM)
    dma = pltpu.SemaphoreType.DMA
    outputs = pl.pallas_call(
        layer_kernel,
        out_shape=(shape(ROWS, ROWS), shape(ROWS, ROWS), shape(ROWS, HD), shape(ROWS, HD)),
        in_specs=[in_smem] + [in_vmem] * 4 + [pl.BlockSpec(memory_space=pl.ANY)],
        out_specs=(in_vmem,) * 4,
        scratch_shapes=[
            half(ROWS, ROWS), half(CTX, 2, ROWS, HD), half(HD, TOKENS), half(HD, TOKENS),
            half(ROWS, ROWS), half(ROWS, ROWS), half(ROWS, ROWS),
            half(4, 2, ROWS, ROWS), half(2, FIRST // CHUNK, 2, CHUNK // 2, ROWS), half(2, 2, FIRST, ROWS),
            half(FIRST, ROWS), half(FIRST, ROWS), half(4, rest, ROWS), half(2, half_b, ROWS),
            half(2, rest, ROWS), half(ROWS, ROWS),
            half(4, HD, wide), half(4, wide, HD), half(4, HD, wide), half(4, wide, HD),
            full(4, HD, wide), full(4, 1, wide), full(4, 1, wide), half(4, HD, wide), full(4, 1, wide), full(4, 1, wide),
            full(4, HD, wide), full(CTX, 2, ROWS, HD),
            half(4, 2, ROWS, ROWS), full(ROWS, ROWS), half(ROWS, ROWS),
            half(8, 2, ROWS, HD), half(8, 2, ROWS, HD), half(8, 2, ROWS, HD),
            half(2, 2, 2, ROWS // 2, HD), half(2, 2, 2, ROWS, HD), half(2, ROWS, HD), half(2, ROWS, HD),
            dma((96,)), dma((96,)),
        ] + [dma((4,))] * 8 + [half(QH * HD, ROWS), dma],
        compiler_params=pltpu.CompilerParams(
            collective_id=0, has_side_effects=True, vmem_limit_bytes=62 << 20
        ),
        name="layer",
    )(lengths, queries, key_input, value_input, grad_projected, out_weight)
    return pl.pallas_call(
        hand_over,
        out_shape=(shape(ROWS, ROWS), shape(ROWS, ROWS), shape(ROWS, HD), shape(ROWS, HD)),
        in_specs=[in_vmem] * 4,
        out_specs=(in_vmem,) * 4,
        name="hand_over",
    )(*outputs)


def solution(mesh):
    both = P("ctx", "head")
    return jax.shard_map(
        body,
        mesh=mesh,
        in_specs=(both, both, both, P(None, "head"), P(), both),
        out_specs=(both, both, both, both),
        check_vma=False,
    )
```
